512 devices in a mesh: agent: 4 (over x_hi, core), expert: 128 (over y, x_lo, z).
Axes of the slice: x: 4 (x_hi: 2, x_lo: 2; x = x_hi * 2 + x_lo), y: 4, z: 16, core: 2. Of those that a mesh axis runs over, the one named last changes fastest.
Arguments:
- expert_ids: int32 [4, 16384, 8], P('agent', 'expert'), may hold values from 0 to 127, all different within a row; in each aligned block of 128 rows (0 to 127, 128 to 255, ..., all dimensions but the last counted through in order) at most 12 rows name the same one
- gate_probs: float32 [4, 16384, 8], P('agent', 'expert'), may hold values from 0.03 to 0.3
- cotangent: bfloat16 [4, 16384, 1024], P('agent', 'expert'), may hold values from -0.19921875 to 0.19921875
- hidden: bfloat16 [4, 128, 1536, 384], P('agent', 'expert'), may hold values from -6 to 6
- w_down: bfloat16 [4, 128, 384, 1024], P('agent', 'expert'), may hold values from -0.3125 to 0.3125
- psi_prev: bfloat16 [4, 128, 384, 1024], P('agent', 'expert'), may hold values from -0.3125 to 0.3125
Outputs:
- mixed_out: bfloat16 [4, 16384, 1024], P('agent', 'expert')
- prob_grad: float32 [4, 16384, 8], P('agent', 'expert')
- w_next: bfloat16 [4, 128, 384, 1024], P('agent', 'expert')
- psi_next: bfloat16 [4, 128, 384, 1024], P('agent', 'expert')
The draws below stay inside these ranges and needn't reach their ends.
Inputs may be any that keep to these rules, and one draw needn't show every extreme that they name: `expert_ids`: each token names 8 different experts. Among the tokens of one device (aligned blocks of 128 rows, agents then tokens) no expert is named more than 12 times, and some expert reaches it.
All inputs are finite; a program needn't handle non-finite values.
Results may differ from the reference program's by a relative error of at most 0.008.
Values may be sent and summed in bfloat16 or wider, within the bound.
A program may use at most 64 MiB of HBM per device.

```python
import math
import jax
import jax.numpy as jnp
import numpy as np
from jax import lax

D = 1024
H = 384
TOPK = 8
TOK_DEV = 128
EXPERTS = 128
CAP_PAIR = 12
SLOTS_E = 1536
TOKENS = 16384
AGENTS = 4
N_AGENT = 4


def block_scale(own_key, shape, shards, least, top_value):
    loudness = 1.0
    for position, blocks in shards:
        steps = jax.random.uniform(jax.random.fold_in(jax.random.fold_in(own_key, 6), position), (blocks,), jnp.float32, least / len(shards), top_value / len(shards))
        loudness = loudness * jnp.repeat(jnp.exp(steps), shape[position] // blocks).reshape((-1,) + (1,) * (len(shape) - 1 - position))
    return loudness


def shared_out(own_key, own, number, rows, count, top, bound, lean):
    order = jax.random.permutation(own_key, count)
    heavy_load, common = shares(count, rows * top, bound, lean, True), shares(count, rows * top, bound, lean, False)
    places = jnp.arange(count)

    def named(tallies, offset_by):
        used = int((tallies > 0).sum())
        fixed = max(1, used // 4)
        passed = fixed + (places - fixed + offset_by * (used - fixed)) % max(1, count - fixed)
        return jnp.zeros((count,), jnp.int32).at[order[jnp.where(places < fixed, places, passed)]].set(jnp.asarray(tallies, jnp.int32))

    tallies = jnp.where(number % 4 == 0, named(heavy_load, number // 4), named(common, number - number // 4 - 1))
    mixed = jax.random.permutation(jax.random.fold_in(own, 3), count)
    source_of, sink = mixed[0:count // 2 * 2:2], mixed[1:count // 2 * 2:2]
    slack = jnp.minimum(tallies[source_of] - 1, bound - tallies[sink]) // 2
    slack = jnp.where((source_of == order[0]) | (sink == order[0]) | (tallies[sink] == 0), 0, jnp.maximum(slack, 0))
    passed = jax.random.randint(jax.random.fold_in(own, 4), (count // 2,), 0, 1 << 20) % (slack + 1)
    tallies = tallies.at[source_of].add(-passed).at[sink].add(passed)
    members = jnp.searchsorted(jnp.cumsum(tallies), jnp.arange(rows * top), side="right").astype(jnp.int32)
    listing = members.reshape(top, rows).T
    listing = listing[jax.random.permutation(jax.random.fold_in(own, 1), rows)]
    offset_by = jax.random.randint(jax.random.fold_in(own, 2), (rows, 1), 0, top)
    return jnp.take_along_axis(listing, (jnp.arange(top)[None, :] + offset_by) % top, axis=1)


def shares(amount, total, limit, skew, full):
    loads = [(1 << 20) // math.isqrt(grade ** skew) + 1 for grade in range(1, amount + 1)]
    largest = limit if full else min(limit, max(-(-total // amount), total * loads[0] // sum(loads)))
    least = 1 if total - largest >= amount - 1 else 0
    counts, surplus = [largest] + [least] * (amount - 1), total - largest - least * (amount - 1)
    while surplus > 0:
        candidates = [i for i in range(1, amount) if counts[i] < largest] or [i for i in range(1, amount) if counts[i] < limit]
        mass, left = sum([loads[i] for i in candidates]), surplus
        for i in candidates:
            addition = min(limit - counts[i], max(1, left * loads[i] // mass), surplus)
            counts[i] = counts[i] + addition
            surplus = surplus - addition
    return np.array(counts)


def noise(stream_key, shape, deviation, bound, shards=(), kind=jnp.bfloat16):
    level = block_scale(stream_key, shape, shards, -0.22, 0.18) if shards else 1.0
    array = jax.random.normal(stream_key, shape, jnp.float32) * deviation * level
    return jnp.minimum(jnp.maximum(array, -bound), bound).astype(kind)


def setup_inputs(seed: int = 0) -> dict:
    streams_of = jax.random.split(jax.random.key(seed), 7)
    expert_ids_keys = jax.random.split(jax.random.fold_in(streams_of[0], 1), AGENTS * TOKENS // TOK_DEV)
    expert_ids_turns = jax.random.permutation(jax.random.fold_in(streams_of[0], 3), AGENTS * TOKENS // TOK_DEV)
    expert_ids = jax.vmap(lambda own, number: shared_out(jax.random.fold_in(streams_of[0], 2), own, number, TOK_DEV, EXPERTS, TOPK, CAP_PAIR, 1))(expert_ids_keys, expert_ids_turns).reshape((AGENTS, TOKENS, TOPK))
    gate_probs = jnp.clip(jnp.exp(math.log(0.3) - 2.3025852 * jax.random.uniform(streams_of[1], (AGENTS, TOKENS, TOPK), jnp.float32) ** block_scale(streams_of[1], (AGENTS, TOKENS, TOPK), ((0, 4), (1, 128)), -0.2, 0.2)), 0.03, 0.3)
    cotangent = noise(streams_of[2], (AGENTS, TOKENS, D), 0.03125, 0.19921875, ((0, 4), (1, 128)))
    hidden = noise(streams_of[3], (AGENTS, EXPERTS, SLOTS_E, H), 1.0, 6.0, ((0, 4), (1, 128)))
    w_down = noise(streams_of[4], (AGENTS, EXPERTS, H, D), H ** -0.5, 0.3125, ((0, 4), (1, 128)))
    psi_prev = noise(streams_of[5], (AGENTS, EXPERTS, H, D), H ** -0.5, 0.3125, ((0, 4), (1, 128)))
    return {"expert_ids": expert_ids, "gate_probs": gate_probs, "cotangent": cotangent, "hidden": hidden, "w_down": w_down, "psi_prev": psi_prev}


step_rate = 0.25


def slot_ranks(choices, col_count):
    marks_hot = (choices[:, None] == jnp.arange(col_count, dtype=jnp.int32)[None, :]).astype(jnp.int32)
    running = jnp.cumsum(marks_hot, axis=0)
    return (jnp.sum(marks_hot * running, axis=1) - 1).astype(jnp.int32)


def one_agent(expert_ids, gate_probs, cotangent, hidden, w_down, psi_prev):
    expert_count = w_down.shape[0]
    sources = expert_ids.shape[0] // TOK_DEV
    per_src = expert_ids.reshape(sources, TOK_DEV * TOPK)
    slot_rank = jax.vmap(lambda row_ids: slot_ranks(row_ids, expert_count))(per_src)
    slot_idx = (jnp.arange(sources, dtype=jnp.int32)[:, None] * CAP_PAIR + slot_rank).astype(jnp.int32)
    outputs = lax.map(lambda operands: jnp.dot(operands[0], operands[1], preferred_element_type=jnp.float32).astype(jnp.bfloat16), (hidden, w_down))
    gate_share = gate_probs.reshape(sources, TOK_DEV, TOPK)
    incoming = cotangent.reshape(sources, TOK_DEV, D)

    def combine(operands):
        row_ids, row_slots, weights_k, grad_rows = operands
        picked = outputs[row_ids, row_slots].astype(jnp.float32).reshape(TOK_DEV, TOPK, D)
        mixed_rows = jnp.sum(weights_k[:, :, None] * picked, axis=1).astype(jnp.bfloat16)
        score_rows = jnp.sum(grad_rows.astype(jnp.float32)[:, None, :] * picked, axis=2)
        return mixed_rows, score_rows

    mixed_out, prob_grad = lax.map(combine, (per_src, slot_idx, gate_share, incoming))

    def place(buffer, operands):
        row_ids, row_slots, weights_k, grad_rows = operands
        scaled = (weights_k[:, :, None] * grad_rows.astype(jnp.float32)[:, None, :]).astype(jnp.bfloat16)
        return buffer.at[row_ids, row_slots].set(scaled.reshape(TOK_DEV * TOPK, D)), None

    placed, unused = lax.scan(place, jnp.zeros((expert_count, SLOTS_E, D), jnp.bfloat16), (per_src, slot_idx, gate_share, incoming))
    gradient = lax.map(lambda operands: lax.dot_general(operands[0], operands[1], (((0,), (0,)), ((), ())), preferred_element_type=jnp.float32), (hidden, placed))
    weight_f = w_down.astype(jnp.float32)
    psi_next = (weight_f - step_rate * gradient).astype(jnp.bfloat16)
    own_phi = psi_next.astype(jnp.float32) + (weight_f - psi_prev.astype(jnp.float32))
    return mixed_out.reshape(-1, D), prob_grad.reshape(-1, TOPK), own_phi, psi_next


def reference(expert_ids, gate_probs, cotangent, hidden, w_down, psi_prev):
    results = [one_agent(expert_ids[agent_idx], gate_probs[agent_idx], cotangent[agent_idx], hidden[agent_idx], w_down[agent_idx], psi_prev[agent_idx]) for agent_idx in range(N_AGENT)]
    mixed_out = jnp.stack([entry[0] for entry in results])
    prob_grad = jnp.stack([entry[1] for entry in results])
    w_next = jnp.stack([(0.5 * (results[agent_idx][2] + results[agent_idx ^ 2][2])).astype(jnp.bfloat16) for agent_idx in range(N_AGENT)])
    psi_next = jnp.stack([entry[3] for entry in results])
    return mixed_out, prob_grad, w_next, psi_next
```

```python
import jax
import jax.numpy as jnp
from jax import lax
from jax.experimental import pallas as pl
from jax.experimental.pallas import tpu as pltpu
from jax.sharding import PartitionSpec as P

Z, Y, X = 16, 4, 2
Q = Y * X
BATCH = 4
BATCHES = Z // BATCH
HALF = Z // 2
STEP_RATE = 0.25
BF, F32 = jnp.bfloat16, jnp.float32


def kernel(
    ids_ref, gates_ref, cot_ref, hidden_ref, weight_ref, prev_ref,
    mixed_ref, prob_ref, next_ref, psi_ref,
    cbuf, meta, prod, rbuf, obuf, rx, mt, key_buf, part, pg, rs_out, rs_in, pg_out, pg_in, phi, phi_out, phi_in,
    ag_send, ag_recv, meta_send, meta_recv, r_send, r_recv, o_send, o_recv,
    rs_send, rs_recv, pg_send, pg_recv, phi_send, phi_recv,
):
    tok, width = cot_ref.shape
    top = ids_ref.shape[0]
    cap = hidden_ref.shape[0] // (Q * Z)
    rows = BATCH * cap
    half = tok // 2
    agent = lax.axis_index("agent")
    me = lax.axis_index("expert")
    z = lax.rem(me, Z)
    column = lax.div(me, Z)
    x = lax.rem(column, X)
    y = lax.div(column, X)

    def on_ring(offset):
        return {"expert": column * Z + lax.rem(z + offset + Z, Z)}

    def peer_column(p):
        dy, dx = p // X, p % X
        return lax.rem(y + dy, Y) * X + lax.rem(x + dx, X)

    def in_plane(p):
        return {"expert": peer_column(p) * Z + z}

    partner = {"agent": lax.rem(agent + 2, 4)}

    def block(offset):
        return lax.rem(z + offset + 2 * Z, Z)

    barrier = pltpu.get_barrier_semaphore()
    peers = [on_ring(1), on_ring(-1), partner] + [in_plane(p) for p in range(1, Q)]
    for peer in peers:
        pl.semaphore_signal(barrier, inc=1, device_id=peer, device_id_type=pl.DeviceIdType.MESH)
    pl.semaphore_wait(barrier, len(peers))

    def remote(src, dst, send, recv, peer):
        return pltpu.make_async_remote_copy(
            src_ref=src, dst_ref=dst, send_sem=send, recv_sem=recv, device_id=peer,
            device_id_type=pl.DeviceIdType.MESH,
        )

    def gather_copy(way, step, piece):
        there = block(-(step - 1) if way == 0 else step - 1)
        place = cbuf.at[there, pl.ds(piece * half, half), :]
        src = cot_ref.at[pl.ds(piece * half, half), :] if step == 1 else place
        return remote(src, place, ag_send.at[way, step - 1, piece], ag_recv.at[way, step - 1, piece],
                      on_ring(1 if way == 0 else -1))

    def meta_copy(way, step):
        place = meta.at[block(-(step - 1) if way == 0 else step - 1)]
        return remote(place, place, meta_send.at[way, step - 1], meta_recv.at[way, step - 1],
                      on_ring(1 if way == 0 else -1))

    def gather_pieces(step):
        if step == HALF:
            return [(0, 0), (1, 1)]
        return [(0, 0), (1, 1), (0, 1), (1, 0)]

    def meta_ways(step):
        return [0] if step == HALF else [0, 1]

    def gather_step(step):
        for way in meta_ways(step):
            if step > 1:
                meta_copy(way, step - 1).wait_recv()
            meta_copy(way, step).start()
        for way, piece in gather_pieces(step):
            if step > 1:
                gather_copy(way, step - 1, piece).wait_recv()
            gather_copy(way, step, piece).start()
        if step > 1:
            for way, piece in gather_pieces(step - 1):
                if (way, piece) not in gather_pieces(step):
                    gather_copy(way, step - 1, piece).wait_recv()
            for way in meta_ways(step - 1):
                if way not in meta_ways(step):
                    meta_copy(way, step - 1).wait_recv()

    meta[z, 0:top, :] = ids_ref[...].astype(F32)
    meta[z, top:2 * top, :] = gates_ref[...]
    gather_step(1)
    cbuf[z] = cot_ref[...]

    def rows_copy(p):
        return remote(prod.at[peer_column(p)], rbuf.at[column], r_send.at[p], r_recv.at[p], in_plane(p))

    def produce(p):
        there = peer_column(p)
        start = pl.multiple_of(there * Z * cap, Z * cap)
        out = jnp.dot(hidden_ref[pl.ds(start, Z * cap), :], weight_ref[...], preferred_element_type=F32).astype(BF)
        if p == 0:
            rbuf[column] = out
        else:
            prod[there] = out
            rows_copy(p).start()

    for p in list(range(1, Q)) + [0]:
        produce(p)

    lane = lax.broadcasted_iota(jnp.int32, (tok, tok), 1)
    sub = lax.broadcasted_iota(jnp.int32, (tok, tok), 0)
    earlier = (sub < lane).astype(F32).astype(BF)
    expert_of = (lax.broadcasted_iota(jnp.int32, (Q, tok), 0) * Z + z).astype(F32)
    row_of = lax.broadcasted_iota(jnp.int32, (rows, tok), 0).astype(F32)

    near = 1 - 2 * lax.div(3 - lax.rem(z, BATCH), 2)
    first = lax.div(z, BATCH)

    def batch_at(order):
        shift = [0, near, -near, 2][order]
        return lax.rem(first + shift + BATCHES, BATCHES)

    def slots(order):
        return pl.ds(pl.multiple_of(batch_at(order) * rows, rows), rows)

    def out_copy(order, p):
        return remote(obuf.at[peer_column(p), slots(order), :], rx.at[column, slots(order), :],
                      o_send.at[order, p], o_recv.at[order, p], in_plane(p))

    def select(order):
        batch = batch_at(order)
        named, weights = [], []
        for i in range(BATCH):
            ids = meta[batch * BATCH + i, 0:top, :]
            gates = meta[batch * BATCH + i, top:2 * top, :]
            hit = jnp.zeros((Q, tok), F32)
            share = jnp.zeros((Q, tok), F32)
            for k in range(top):
                same = ids[k:k + 1, :] == expert_of
                hit = hit + jnp.where(same, 1.0, 0.0)
                share = share + jnp.where(same, gates[k:k + 1, :], 0.0)
            named.append(hit)
            weights.append(share)
        rank = jnp.dot(jnp.concatenate(named, axis=0).astype(BF), earlier, preferred_element_type=F32)
        for i in range(BATCH):
            key = jnp.where(named[i] > 0.5, rank[i * Q:(i + 1) * Q, :] + float(i * cap), -1.0)
            key_buf[batch * BATCH + i] = key
            for q in range(Q):
                chosen = jnp.where(row_of == key[q:q + 1, :], weights[i][q:q + 1, :], 0.0)
                mt[batch, pl.ds(q * rows, rows), pl.ds(i * tok, tok)] = chosen.astype(BF)

    def dispatch(order):
        batch = batch_at(order)
        select(order)

        def chunk(n, carry):
            cols = pl.ds(pl.multiple_of(n * 256, 256), 256)
            tokens = cbuf[pl.ds(batch * BATCH, BATCH), :, cols].reshape(BATCH * tok, 256)
            out = jnp.dot(mt[batch], tokens, preferred_element_type=F32).astype(BF)
            obuf[:, slots(order), cols] = out.reshape(Q, rows, 256)
            return carry

        lax.fori_loop(0, width // 256, chunk, 0)
        for p in range(1, Q):
            out_copy(order, p).start()
        rx[column, slots(order), :] = obuf[column, slots(order), :]

    def combine(order):
        batch = batch_at(order)

        def chunk(n, carry):
            cols = pl.ds(pl.multiple_of(n * 256, 256), 256)
            arrived = rbuf[:, slots(order), cols].reshape(Q * rows, 256)
            out = lax.dot_general(mt[batch], arrived, (((0,), (0,)), ((), ())), preferred_element_type=F32)
            part[pl.ds(batch * BATCH, BATCH), :, cols] = out.reshape(BATCH, tok, 256)
            return carry

        lax.fori_loop(0, width // 256, chunk, 0)
        for i in range(BATCH):
            source = batch * BATCH + i
            scores = lax.dot_general(
                rbuf[:, slots(order), :].reshape(Q * rows, width), cbuf[source],
                (((1,), (1,)), ((), ())), preferred_element_type=F32,
            )
            key = key_buf[source]
            ids = meta[source, 0:top, :]
            total = jnp.zeros((top, tok), F32)
            for q in range(Q):
                picked = jnp.where(row_of == key[q:q + 1, :], scores[q * rows:(q + 1) * rows, :], 0.0)
                value = jnp.sum(picked, axis=0, keepdims=True)
                total = total + jnp.where(ids == (z + q * Z).astype(F32), value, 0.0)
            pg[source] = total

    gather_step(2)
    gather_step(3)
    gather_step(4)
    dispatch(0)
    gather_step(5)
    gather_step(6)
    dispatch(1)
    gather_step(7)
    gather_step(8)
    dispatch(2)
    for p in range(1, Q):
        rows_copy(p).wait_recv()
    for order in range(3):
        combine(order)
    for way in meta_ways(HALF):
        meta_copy(way, HALF).wait_recv()
    for way, piece in gather_pieces(HALF):
        gather_copy(way, HALF, piece).wait_recv()
    dispatch(3)
    combine(3)

    def scatter_copy(way, step, piece):
        span = pl.ds(piece * half, half)
        return remote(rs_out.at[way, step - 1, span, :], rs_in.at[way, step - 1, span, :],
                      rs_send.at[way, step - 1, piece], rs_recv.at[way, step - 1, piece],
                      on_ring(1 if way == 0 else -1))

    def pg_copy(way, step):
        return remote(pg_out.at[way, step - 1], pg_in.at[way, step - 1], pg_send.at[way, step - 1],
                      pg_recv.at[way, step - 1], on_ring(1 if way == 0 else -1))

    def scatter_pieces(step):
        return [(0, 0), (1, 1)] if step == 1 else [(0, 0), (1, 1), (0, 1), (1, 0)]

    def pg_ways(step):
        return [0] if step == 1 else [0, 1]

    def scatter_step(step):
        for way, piece in scatter_pieces(step):
            there = block(HALF + 1 - step if way == 0 else step - HALF - 1)
            span = pl.ds(piece * half, half)
            value = part[there, span, :]
            if (way, piece) in scatter_pieces(step - 1) and step > 1:
                scatter_copy(way, step - 1, piece).wait_recv()
                value = value + rs_in[way, step - 2, span, :].astype(F32)
            rs_out[way, step - 1, span, :] = value.astype(BF)
            scatter_copy(way, step, piece).start()
        for way in pg_ways(step):
            there = block(HALF + 1 - step if way == 0 else step - HALF - 1)
            value = pg[there]
            if step > 1 and way in pg_ways(step - 1):
                pg_copy(way, step - 1).wait_recv()
                value = value + pg_in[way, step - 2]
            pg_out[way, step - 1] = value
            pg_copy(way, step).start()

    def phi_copy(i):
        span = pl.ds(i * 128, 128)
        return remote(phi_out.at[span, :], phi_in.at[span, :], phi_send.at[i], phi_recv.at[i], partner)

    phis = hidden_ref.shape[1] // 128
    scatter_step(1)
    scatter_step(2)
    scatter_step(3)
    for order in range(BATCHES):
        for p in range(1, Q):
            out_copy(order, p).wait_recv()
    for i in range(phis):
        span = pl.ds(i * 128, 128)
        gradient = lax.dot_general(
            hidden_ref[:, span], rx[...].reshape(Q * Z * cap, width), (((0,), (0,)), ((), ())),
            preferred_element_type=F32,
        )
        weight = weight_ref[span, :].astype(F32)
        psi = (weight - STEP_RATE * gradient).astype(BF)
        psi_ref[span, :] = psi
        own = psi.astype(F32) + (weight - prev_ref[span, :].astype(F32))
        phi[span, :] = own
        phi_out[span, :] = own.astype(BF)
        phi_copy(i).start()
    for step in range(4, HALF + 1):
        scatter_step(step)
    for i in range(phis):
        span = pl.ds(i * 128, 128)
        phi_copy(i).wait_recv()
        next_ref[span, :] = (0.5 * (phi[span, :] + phi_in[span, :].astype(F32))).astype(BF)
    for way, piece in scatter_pieces(HALF):
        scatter_copy(way, HALF, piece).wait_recv()
    for way in pg_ways(HALF):
        pg_copy(way, HALF).wait_recv()
    mixed_ref[...] = (
        part[z] + rs_in[0, HALF - 1].astype(F32) + rs_in[1, HALF - 1].astype(F32)
    ).astype(BF)
    prob_ref[...] = pg[z] + pg_in[0, HALF - 1] + pg_in[1, HALF - 1]

    for step in range(1, HALF + 1):
        for way, piece in gather_pieces(step):
            gather_copy(way, step, piece).wait_send()
        for way in meta_ways(step):
            meta_copy(way, step).wait_send()
        for way, piece in scatter_pieces(step):
            scatter_copy(way, step, piece).wait_send()
        for way in pg_ways(step):
            pg_copy(way, step).wait_send()
    for p in range(1, Q):
        rows_copy(p).wait_send()
        for order in range(BATCHES):
            out_copy(order, p).wait_send()
    for i in range(phis):
        phi_copy(i).wait_send()


def per_device(expert_ids, gate_probs, cotangent, hidden, w_down, psi_prev):
    tok, top = expert_ids.shape[1:]
    width = cotangent.shape[2]
    slot_count, inner = hidden.shape[2:]
    cap = slot_count // (Q * Z)
    rows = BATCH * cap
    vmem = pl.BlockSpec(memory_space=pltpu.VMEM)
    dma = pltpu.SemaphoreType.DMA
    mixed, prob, w_next, psi_next = pl.pallas_call(
        kernel,
        out_shape=(
            jax.ShapeDtypeStruct((tok, width), BF),
            jax.ShapeDtypeStruct((top, tok), F32),
            jax.ShapeDtypeStruct((inner, width), BF),
            jax.ShapeDtypeStruct((inner, width), BF),
        ),
        in_specs=[vmem] * 6,
        out_specs=(vmem,) * 4,
        scratch_shapes=[
            pltpu.VMEM((Z, tok, width), BF),
            pltpu.VMEM((Z, 2 * top, tok), F32),
            pltpu.VMEM((Q, Z * cap, width), BF),
            pltpu.VMEM((Q, Z * cap, width), BF),
            pltpu.VMEM((Q, Z * cap, width), BF),
            pltpu.VMEM((Q, Z * cap, width), BF),
            pltpu.VMEM((BATCHES, Q * rows, BATCH * tok), BF),
            pltpu.VMEM((Z, Q, tok), F32),
            pltpu.VMEM((Z, tok, width), F32),
            pltpu.VMEM((Z, top, tok), F32),
            pltpu.VMEM((2, HALF, tok, width), BF),
            pltpu.VMEM((2, HALF, tok, width), BF),
            pltpu.VMEM((2, HALF, top, tok), F32),
            pltpu.VMEM((2, HALF, top, tok), F32),
            pltpu.VMEM((inner, width), F32),
            pltpu.VMEM((inner, width), BF),
            pltpu.VMEM((inner, width), BF),
            dma((2, HALF, 2)), dma((2, HALF, 2)),
            dma((2, HALF)), dma((2, HALF)),
            dma((Q,)), dma((Q,)),
            dma((BATCHES, Q)), dma((BATCHES, Q)),
            dma((2, HALF, 2)), dma((2, HALF, 2)),
            dma((2, HALF)), dma((2, HALF)),
            dma((inner // 128,)), dma((inner // 128,)),
        ],
        compiler_params=pltpu.CompilerParams(
            collective_id=0, has_side_effects=True, vmem_limit_bytes=60 * 1024 * 1024,
        ),
    )(expert_ids[0].T, gate_probs[0].T, cotangent[0], hidden[0, 0], w_down[0, 0], psi_prev[0, 0])
    return mixed[None], prob.T[None], w_next[None, None], psi_next[None, None]


def solution(mesh):
    return jax.shard_map(
        per_device,
        mesh=mesh,
        in_specs=(
            P("agent", "expert", None),
            P("agent", "expert", None),
            P("agent", "expert", None),
            P("agent", "expert", None, None),
            P("agent", "expert", None, None),
            P("agent", "expert", None, None),
        ),
        out_specs=(
            P("agent", "expert", None),
            P("agent", "expert", None),
            P("agent", "expert", None, None),
            P("agent", "expert", None, None),
        ),
        check_vma=False,
    )
```

```python
import jax
import jax.numpy as jnp
from jax import lax
from jax.experimental import pallas as pl
from jax.experimental.pallas import tpu as pltpu
from jax.sharding import PartitionSpec as P

Z, Y, X = 16, 4, 2
Q = Y * X
BATCH = 4
BATCHES = Z // BATCH
HALF = Z // 2
STEP_RATE = 0.25
BF, F32 = jnp.bfloat16, jnp.float32


def kernel(
    ids_ref, gates_ref, cot_ref, hidden_hbm, weight_hbm, prev_hbm,
    mixed_ref, prob_ref, next_hbm, psi_hbm,
    cbuf, meta, prod, rbuf, obuf, rx, mt, mtt, key_buf, part, pg, rs_out, rs_in, pg_out, pg_in, phi, phi_out, phi_in,
    hidden_ref, weight_ref, prev_ref, next_ref, psi_ref,
    ag_send, ag_recv, meta_send, meta_recv, r_send, r_recv, o_send, o_recv,
    rs_send, rs_recv, pg_send, pg_recv, phi_send, phi_recv, local_sem,
):
    tok, width = cot_ref.shape
    top = ids_ref.shape[0]
    cap = hidden_ref.shape[0] // (Q * Z)
    rows = BATCH * cap
    half = tok // 2
    side = width // 2
    agent = lax.axis_index("agent")
    me = lax.axis_index("expert")
    z = lax.rem(me, Z)
    column = lax.div(me, Z)
    x = lax.rem(column, X)
    y = lax.div(column, X)

    def on_ring(offset):
        return {"expert": column * Z + lax.rem(z + offset + Z, Z)}

    def peer_column(p):
        dy, dx = p // X, p % X
        return lax.rem(y + dy, Y) * X + lax.rem(x + dx, X)

    def in_plane(p):
        return {"expert": peer_column(p) * Z + z}

    partner = {"agent": lax.rem(agent + 2, 4)}

    def block(offset):
        return lax.rem(z + offset + 2 * Z, Z)

    barrier = pltpu.get_barrier_semaphore()
    peers = [on_ring(1), on_ring(-1), partner] + [in_plane(p) for p in range(1, Q)]
    for peer in peers:
        pl.semaphore_signal(barrier, inc=1, device_id=peer, device_id_type=pl.DeviceIdType.MESH)

    loads = [
        pltpu.make_async_copy(src, dst, local_sem.at[i])
        for i, (src, dst) in enumerate([
            (hidden_hbm, hidden_ref), (weight_hbm, weight_ref), (cot_ref, cbuf.at[z]), (prev_hbm, prev_ref),
        ])
    ]
    for load in loads:
        load.start()
    meta[z, 0:top, :] = ids_ref[...].astype(F32).astype(BF)
    meta[z, top:2 * top, :] = gates_ref[...].astype(BF)
    pl.semaphore_wait(barrier, len(peers))

    def remote(src, dst, send, recv, peer):
        return pltpu.make_async_remote_copy(
            src_ref=src, dst_ref=dst, send_sem=send, recv_sem=recv, device_id=peer,
            device_id_type=pl.DeviceIdType.MESH,
        )

    def gather_copy(way, step, piece):
        there = block(-(step - 1) if way == 0 else step - 1)
        place = cbuf.at[there, pl.ds(piece * half, half), :]
        src = cot_ref.at[pl.ds(piece * half, half), :] if step == 1 else place
        return remote(src, place, ag_send.at[way, step - 1, piece], ag_recv.at[way, step - 1, piece],
                      on_ring(1 if way == 0 else -1))

    def meta_copy(way, step):
        place = meta.at[block(-(step - 1) if way == 0 else step - 1)]
        return remote(place, place, meta_send.at[way, step - 1], meta_recv.at[way, step - 1],
                      on_ring(1 if way == 0 else -1))

    def gather_pieces(step):
        if step == HALF:
            return [(0, 0), (1, 1)]
        return [(0, 0), (1, 1), (0, 1), (1, 0)]

    def meta_ways(step):
        return [0] if step == HALF else [0, 1]

    def gather_step(step):
        for way in meta_ways(step):
            if step > 1:
                meta_copy(way, step - 1).wait_recv()
            meta_copy(way, step).start()
        for way, piece in gather_pieces(step):
            if step > 1:
                gather_copy(way, step - 1, piece).wait_recv()
            gather_copy(way, step, piece).start()
        if step > 1:
            for way, piece in gather_pieces(step - 1):
                if (way, piece) not in gather_pieces(step):
                    gather_copy(way, step - 1, piece).wait_recv()
            for way in meta_ways(step - 1):
                if way not in meta_ways(step):
                    meta_copy(way, step - 1).wait_recv()

    gather_step(1)
    loads[0].wait()
    loads[1].wait()

    def rows_copy(p):
        return remote(prod.at[peer_column(p)], rbuf.at[column], r_send.at[p], r_recv.at[p], in_plane(p))

    def produce(p):
        there = peer_column(p)
        start = pl.multiple_of(there * Z * cap, Z * cap)
        out = jnp.dot(hidden_ref[pl.ds(start, Z * cap), :], weight_ref[...], preferred_element_type=F32).astype(BF)
        if p == 0:
            rbuf[column] = out
        else:
            prod[there] = out
            rows_copy(p).start()

    for p in list(range(1, Q)) + [0]:
        produce(p)

    lane = lax.broadcasted_iota(jnp.int32, (tok, tok), 1)
    sub = lax.broadcasted_iota(jnp.int32, (tok, tok), 0)
    earlier = (sub < lane).astype(F32).astype(BF)
    expert_of = (lax.broadcasted_iota(jnp.int32, (Q, tok), 0) * Z + z).astype(F32)
    row_of = lax.broadcasted_iota(jnp.int32, (rows, tok), 0).astype(F32)

    near = 1 - 2 * lax.div(3 - lax.rem(z, BATCH), 2)
    first = lax.div(z, BATCH)

    def batch_at(order):
        shift = [0, near, -near, 2][order]
        return lax.rem(first + shift + BATCHES, BATCHES)

    def slots(order):
        return pl.ds(pl.multiple_of(batch_at(order) * rows, rows), rows)

    def out_copy(order, p, part_of):
        return remote(obuf.at[part_of, peer_column(p), slots(order), :], rx.at[part_of, column, slots(order), :],
                      o_send.at[part_of, order, p], o_recv.at[part_of, order, p], in_plane(p))

    def select(order):
        batch = batch_at(order)
        named, weights = [], []
        for i in range(BATCH):
            about = meta[batch * BATCH + i].astype(F32)
            ids, gates = about[0:top, :], about[top:2 * top, :]
            hit = jnp.zeros((Q, tok), F32)
            share = jnp.zeros((Q, tok), F32)
            for k in range(top):
                same = ids[k:k + 1, :] == expert_of
                hit = hit + jnp.where(same, 1.0, 0.0)
                share = share + jnp.where(same, gates[k:k + 1, :], 0.0)
            named.append(hit)
            weights.append(share)
        rank = jnp.dot(jnp.concatenate(named, axis=0).astype(BF), earlier, preferred_element_type=F32)
        for i in range(BATCH):
            key = jnp.where(named[i] > 0.5, rank[i * Q:(i + 1) * Q, :] + float(i * cap), -1.0)
            key_buf[batch * BATCH + i] = key
            chosen = jnp.concatenate(
                [jnp.where(row_of == key[q:q + 1, :], weights[i][q:q + 1, :], 0.0) for q in range(Q)], axis=0
            )
            mt[batch, :, pl.ds(i * tok, tok)] = chosen.astype(BF)
            mtt[batch, pl.ds(i * tok, tok), :] = chosen.T.astype(BF)

    def build_out(order):
        batch = batch_at(order)

        def chunk(n, carry):
            cols = pl.ds(pl.multiple_of(n * 256, 256), 256)
            tokens = cbuf[pl.ds(batch * BATCH, BATCH), :, cols].reshape(BATCH * tok, 256)
            out = jnp.dot(mt[batch], tokens, preferred_element_type=F32).astype(BF)
            inner = pl.ds(pl.multiple_of(lax.rem(n, side // 256) * 256, 256), 256)
            obuf[lax.div(n, side // 256), :, slots(order), inner] = out.reshape(Q, rows, 256)
            return carry

        lax.fori_loop(0, width // 256, chunk, 0)

    def send_out(order, part_of):
        for p in range(1, Q):
            out_copy(order, p, part_of).start()
        rx[part_of, column, slots(order), :] = obuf[part_of, column, slots(order), :]

    def weigh(order):
        batch = batch_at(order)

        def chunk(n, carry):
            cols = pl.ds(pl.multiple_of(n * 256, 256), 256)
            arrived = rbuf[:, slots(order), cols].reshape(Q * rows, 256)
            out = jnp.dot(mtt[batch], arrived, preferred_element_type=F32)
            part[pl.ds(batch * BATCH, BATCH), :, cols] = out.reshape(BATCH, tok, 256)
            return carry

        lax.fori_loop(0, width // 256, chunk, 0)

    def score(order):
        batch = batch_at(order)
        for i in range(BATCH):
            source = batch * BATCH + i
            scores = lax.dot_general(
                rbuf[:, slots(order), :].reshape(Q * rows, width), cbuf[source],
                (((1,), (1,)), ((), ())), preferred_element_type=F32,
            )
            key = key_buf[source]
            ids = meta[source].astype(F32)[0:top, :]
            total = jnp.zeros((top, tok), F32)
            for q in range(Q):
                picked = jnp.where(row_of == key[q:q + 1, :], scores[q * rows:(q + 1) * rows, :], 0.0)
                value = jnp.sum(picked, axis=0, keepdims=True)
                total = total + jnp.where(ids == (z + q * Z).astype(F32), value, 0.0)
            pg[source] = total

    def scatter_copy(way, step, piece):
        span = pl.ds(piece * half, half)
        return remote(rs_out.at[way, step - 1, span, :], rs_in.at[way, step - 1, span, :],
                      rs_send.at[way, step - 1, piece], rs_recv.at[way, step - 1, piece],
                      on_ring(1 if way == 0 else -1))

    def pg_copy(way, step):
        return remote(pg_out.at[way, step - 1], pg_in.at[way, step - 1], pg_send.at[way, step - 1],
                      pg_recv.at[way, step - 1], on_ring(1 if way == 0 else -1))

    def scatter_pieces(step):
        return [(0, 0), (1, 1)] if step == 1 else [(0, 0), (1, 1), (0, 1), (1, 0)]

    def pg_ways(step):
        return [0] if step == 1 else [0, 1]

    def scatter_step(step):
        for way, piece in scatter_pieces(step):
            there = block(HALF + 1 - step if way == 0 else step - HALF - 1)
            span = pl.ds(piece * half, half)
            value = part[there, span, :]
            if step > 1 and (way, piece) in scatter_pieces(step - 1):
                scatter_copy(way, step - 1, piece).wait_recv()
                value = value + rs_in[way, step - 2, span, :].astype(F32)
            rs_out[way, step - 1, span, :] = value.astype(BF)
            scatter_copy(way, step, piece).start()

    def pg_step(step):
        for way in pg_ways(step):
            there = block(HALF + 1 - step if way == 0 else step - HALF - 1)
            value = pg[there]
            if step > 1 and way in pg_ways(step - 1):
                pg_copy(way, step - 1).wait_recv()
                value = value + pg_in[way, step - 2]
            pg_out[way, step - 1] = value
            pg_copy(way, step).start()

    def phi_copy(part_of):
        return remote(phi_out.at[part_of], phi_in.at[part_of], phi_send.at[part_of], phi_recv.at[part_of], partner)

    inner = hidden_ref.shape[1]

    def psi_store(part_of):
        cols = pl.ds(part_of * side, side)
        return pltpu.make_async_copy(psi_ref.at[:, cols], psi_hbm.at[:, cols], local_sem.at[4 + part_of])

    def next_store(part_of):
        cols = pl.ds(part_of * side, side)
        return pltpu.make_async_copy(next_ref.at[:, cols], next_hbm.at[:, cols], local_sem.at[6 + part_of])

    def update(part_of):
        for order in range(BATCHES):
            for p in range(1, Q):
                out_copy(order, p, part_of).wait_recv()
        cols = pl.ds(part_of * side, side)
        for i in range(inner // 128):
            span = pl.ds(i * 128, 128)
            gradient = lax.dot_general(
                hidden_ref[:, span], rx[part_of].reshape(Q * Z * cap, side), (((0,), (0,)), ((), ())),
                preferred_element_type=F32,
            )
            weight = weight_ref[span, cols].astype(F32)
            psi = (weight - STEP_RATE * gradient).astype(BF)
            psi_ref[span, cols] = psi
            own = psi.astype(F32) + (weight - prev_ref[span, cols].astype(F32))
            phi[part_of, span, :] = own
            phi_out[part_of, span, :] = own.astype(BF)
        phi_copy(part_of).start()
        psi_store(part_of).start()

    def mean(part_of):
        phi_copy(part_of).wait_recv()
        cols = pl.ds(part_of * side, side)
        next_ref[:, cols] = (0.5 * (phi[part_of] + phi_in[part_of].astype(F32))).astype(BF)
        next_store(part_of).start()

    gather_step(2)
    loads[2].wait()
    loads[3].wait()
    gather_step(3)
    gather_step(4)
    select(0)
    build_out(0)
    gather_step(5)
    gather_step(6)
    select(1)
    build_out(1)
    gather_step(7)
    send_out(0, 0)
    send_out(1, 0)
    gather_step(8)
    for way in meta_ways(HALF):
        meta_copy(way, HALF).wait_recv()
    select(3)
    for p in range(1, Q):
        rows_copy(p).wait_recv()
    weigh(3)
    scatter_step(1)
    select(2)
    build_out(2)
    send_out(2, 0)
    for way, piece in gather_pieces(HALF):
        gather_copy(way, HALF, piece).wait_recv()
    build_out(3)
    send_out(3, 0)
    for order in range(BATCHES):
        send_out(order, 1)
    weigh(2)
    scatter_step(2)
    score(3)
    pg_step(1)
    score(2)
    scatter_step(3)
    pg_step(2)
    weigh(1)
    scatter_step(4)
    pg_step(3)
    update(0)
    score(1)
    weigh(0)
    scatter_step(5)
    pg_step(4)
    score(0)
    scatter_step(6)
    pg_step(5)
    scatter_step(7)
    pg_step(6)
    update(1)
    scatter_step(8)
    pg_step(7)
    mean(0)
    pg_step(8)
    mean(1)
    for way, piece in scatter_pieces(HALF):
        scatter_copy(way, HALF, piece).wait_recv()
    for way in pg_ways(HALF):
        pg_copy(way, HALF).wait_recv()
    mixed_ref[...] = (
        part[z] + rs_in[0, HALF - 1].astype(F32) + rs_in[1, HALF - 1].astype(F32)
    ).astype(BF)
    prob_ref[...] = pg[z] + pg_in[0, HALF - 1] + pg_in[1, HALF - 1]

    for step in range(1, HALF + 1):
        for way, piece in gather_pieces(step):
            gather_copy(way, step, piece).wait_send()
        for way in meta_ways(step):
            meta_copy(way, step).wait_send()
        for way, piece in scatter_pieces(step):
            scatter_copy(way, step, piece).wait_send()
        for way in pg_ways(step):
            pg_copy(way, step).wait_send()
    for p in range(1, Q):
        rows_copy(p).wait_send()
        for order in range(BATCHES):
            for part_of in range(2):
                out_copy(order, p, part_of).wait_send()
    for part_of in range(2):
        phi_copy(part_of).wait_send()
        psi_store(part_of).wait()
        next_store(part_of).wait()


def hand_out(*refs):
    count = (len(refs) - 1) // 3
    sem = refs[-1]
    operands, results, held = refs[:count], refs[count:2 * count], refs[2 * count:3 * count]
    into = [pltpu.make_async_copy(operands[i], held[i], sem.at[0, i]) for i in range(count)]
    out = [pltpu.make_async_copy(held[i], results[i], sem.at[1, i]) for i in range(count)]
    for copy in into:
        copy.start()
    for i in range(count):
        into[i].wait()
        out[i].start()
    for copy in out:
        copy.wait()


def per_device(expert_ids, gate_probs, cotangent, hidden, w_down, psi_prev):
    tok, top = expert_ids.shape[1:]
    width = cotangent.shape[2]
    slot_count, inner = hidden.shape[2:]
    cap = slot_count // (Q * Z)
    rows = BATCH * cap
    vmem, anywhere = pl.BlockSpec(memory_space=pltpu.VMEM), pl.BlockSpec(memory_space=pl.ANY)
    dma = pltpu.SemaphoreType.DMA
    shapes = (
        jax.ShapeDtypeStruct((tok, width), BF),
        jax.ShapeDtypeStruct((top, tok), F32),
        jax.ShapeDtypeStruct((inner, width), BF),
        jax.ShapeDtypeStruct((inner, width), BF),
    )
    made = pl.pallas_call(
        kernel,
        out_shape=shapes,
        in_specs=[vmem] * 2 + [anywhere] * 4,
        out_specs=(vmem, vmem, anywhere, anywhere),
        scratch_shapes=[
            pltpu.VMEM((Z, tok, width), BF),
            pltpu.VMEM((Z, 2 * top, tok), BF),
            pltpu.VMEM((Q, Z * cap, width), BF),
            pltpu.VMEM((Q, Z * cap, width), BF),
            pltpu.VMEM((2, Q, Z * cap, width // 2), BF),
            pltpu.VMEM((2, Q, Z * cap, width // 2), BF),
            pltpu.VMEM((BATCHES, Q * rows, BATCH * tok), BF),
            pltpu.VMEM((BATCHES, BATCH * tok, Q * rows), BF),
            pltpu.VMEM((Z, Q, tok), F32),
            pltpu.VMEM((Z, tok, width), F32),
            pltpu.VMEM((Z, top, tok), F32),
            pltpu.VMEM((2, HALF, tok, width), BF),
            pltpu.VMEM((2, HALF, tok, width), BF),
            pltpu.VMEM((2, HALF, top, tok), F32),
            pltpu.VMEM((2, HALF, top, tok), F32),
            pltpu.VMEM((2, inner, width // 2), F32),
            pltpu.VMEM((2, inner, width // 2), BF),
            pltpu.VMEM((2, inner, width // 2), BF),
            pltpu.VMEM((slot_count, inner), BF),
            pltpu.VMEM((inner, width), BF),
            pltpu.VMEM((inner, width), BF),
            pltpu.VMEM((inner, width), BF),
            pltpu.VMEM((inner, width), BF),
            dma((2, HALF, 2)), dma((2, HALF, 2)),
            dma((2, HALF)), dma((2, HALF)),
            dma((Q,)), dma((Q,)),
            dma((2, BATCHES, Q)), dma((2, BATCHES, Q)),
            dma((2, HALF, 2)), dma((2, HALF, 2)),
            dma((2, HALF)), dma((2, HALF)),
            dma((2,)), dma((2,)),
            dma((8,)),
        ],
        compiler_params=pltpu.CompilerParams(
            collective_id=0, has_side_effects=True, vmem_limit_bytes=60 * 1024 * 1024,
        ),
    )(expert_ids[0].T, gate_probs[0].T, cotangent[0], hidden[0, 0], w_down[0, 0], psi_prev[0, 0])
    mixed, prob, w_next, psi_next = pl.pallas_call(
        hand_out,
        out_shape=shapes,
        in_specs=[anywhere] * 4,
        out_specs=(anywhere,) * 4,
        scratch_shapes=[pltpu.VMEM(shape.shape, shape.dtype) for shape in shapes] + [dma((2, 4))],
    )(*made)
    return mixed[None], prob.T[None], w_next[None, None], psi_next[None, None]


def solution(mesh):
    return jax.shard_map(
        per_device,
        mesh=mesh,
        in_specs=(
            P("agent", "expert", None),
            P("agent", "expert", None),
            P("agent", "expert", None),
            P("agent", "expert", None, None),
            P("agent", "expert", None, None),
            P("agent", "expert", None, None),
        ),
        out_specs=(
            P("agent", "expert", None),
            P("agent", "expert", None),
            P("agent", "expert", None, None),
            P("agent", "expert", None, None),
        ),
        check_vma=False,
    )
```

```python
import jax
import jax.numpy as jnp
from jax import lax
from jax.experimental import pallas as pl
from jax.experimental.pallas import tpu as pltpu
from jax.sharding import PartitionSpec as P

Z, Y, X = 16, 4, 2
Q = Y * X
BATCH = 4
BATCHES = Z // BATCH
HALF = Z // 2
STEP_RATE = 0.25
BF, F32 = jnp.bfloat16, jnp.float32


def kernel(
    ids_hbm, gates_hbm, cot_ref, hidden_hbm, weight_hbm, prev_hbm,
    mixed_ref, prob_ref, next_hbm, psi_hbm,
    cbuf, meta, prod, rbuf, obuf, rx, mt, mtt, key_buf, part, pg, rs_out, rs_in, pg_out, pg_in, phi, phi_out, phi_in,
    ids_ref, gates_ref, hidden_ref, weight_ref, prev_ref, next_ref, psi_ref,
    ag_send, ag_recv, meta_send, meta_recv, r_send, r_recv, o_send, o_recv,
    rs_send, rs_recv, pg_send, pg_recv, phi_send, phi_recv, local_sem,
):
    tok, width = cot_ref.shape
    top = ids_hbm.shape[0]
    cap = hidden_ref.shape[0] // (Q * Z)
    rows = BATCH * cap
    half = tok // 2
    side = width // 2
    agent = lax.axis_index("agent")
    me = lax.axis_index("expert")
    z = lax.rem(me, Z)
    column = lax.div(me, Z)
    x = lax.rem(column, X)
    y = lax.div(column, X)

    def on_ring(offset):
        return {"expert": column * Z + lax.rem(z + offset + Z, Z)}

    def peer_column(p):
        dy, dx = p // X, p % X
        return lax.rem(y + dy, Y) * X + lax.rem(x + dx, X)

    def in_plane(p):
        return {"expert": peer_column(p) * Z + z}

    partner = {"agent": lax.rem(agent + 2, 4)}

    def block(offset):
        return lax.rem(z + offset + 2 * Z, Z)

    barrier = pltpu.get_barrier_semaphore()
    peers = [on_ring(1), on_ring(-1), partner] + [in_plane(p) for p in range(1, Q)]
    for peer in peers:
        pl.semaphore_signal(barrier, inc=1, device_id=peer, device_id_type=pl.DeviceIdType.MESH)

    loads = [
        pltpu.make_async_copy(src, dst, local_sem.at[i])
        for i, (src, dst) in enumerate([
            (ids_hbm, ids_ref), (gates_hbm, gates_ref), (hidden_hbm, hidden_ref), (weight_hbm, weight_ref),
            (cot_ref, cbuf.at[z]), (prev_hbm, prev_ref),
        ])
    ]
    for load in loads:
        load.start()
    pl.semaphore_wait(barrier, len(peers))

    def remote(src, dst, send, recv, peer):
        return pltpu.make_async_remote_copy(
            src_ref=src, dst_ref=dst, send_sem=send, recv_sem=recv, device_id=peer,
            device_id_type=pl.DeviceIdType.MESH,
        )

    def gather_copy(way, step, piece):
        there = block(-(step - 1) if way == 0 else step - 1)
        place = cbuf.at[there, pl.ds(piece * half, half), :]
        src = cot_ref.at[pl.ds(piece * half, half), :] if step == 1 else place
        return remote(src, place, ag_send.at[way, step - 1, piece], ag_recv.at[way, step - 1, piece],
                      on_ring(1 if way == 0 else -1))

    def meta_copy(way, step):
        place = meta.at[block(-(step - 1) if way == 0 else step - 1)]
        return remote(place, place, meta_send.at[way, step - 1], meta_recv.at[way, step - 1],
                      on_ring(1 if way == 0 else -1))

    def gather_pieces(step):
        if step == HALF:
            return [(0, 0), (1, 1)]
        return [(0, 0), (1, 1), (0, 1), (1, 0)]

    def meta_ways(step):
        return [0] if step == HALF else [0, 1]

    def meta_hop(way, step):
        if step > 1 and way in meta_ways(step - 1):
            meta_copy(way, step - 1).wait_recv()
        if way in meta_ways(step):
            meta_copy(way, step).start()

    def gather_pair(step, pair, about=0):
        for way in (0, 1):
            piece = way if pair == 0 else 1 - way
            if step > 1:
                gather_copy(way, step - 1, piece).wait_recv()
            if about:
                meta_hop(way, about)
            gather_copy(way, step, piece).start()

    gather_pair(1, 0)
    loads[0].wait()
    loads[1].wait()
    meta[z, 0:top, :] = ids_ref[...].astype(F32).astype(BF)
    meta[z, top:2 * top, :] = gates_ref[...].astype(BF)
    gather_pair(1, 1, about=1)
    loads[2].wait()
    loads[3].wait()

    def rows_copy(p):
        return remote(prod.at[peer_column(p)], rbuf.at[column], r_send.at[p], r_recv.at[p], in_plane(p))

    def produce(p):
        there = peer_column(p)
        start = pl.multiple_of(there * Z * cap, Z * cap)
        out = jnp.dot(hidden_ref[pl.ds(start, Z * cap), :], weight_ref[...], preferred_element_type=F32).astype(BF)
        if p == 0:
            rbuf[column] = out
        else:
            prod[there] = out
            rows_copy(p).start()

    for p in list(range(1, Q)) + [0]:
        produce(p)

    lane = lax.broadcasted_iota(jnp.int32, (tok, tok), 1)
    sub = lax.broadcasted_iota(jnp.int32, (tok, tok), 0)
    earlier = (sub < lane).astype(F32).astype(BF)
    expert_of = (lax.broadcasted_iota(jnp.int32, (Q, tok), 0) * Z + z).astype(F32)
    row_of = lax.broadcasted_iota(jnp.int32, (rows, tok), 0).astype(F32)

    near = 1 - 2 * lax.div(3 - lax.rem(z, BATCH), 2)
    first = lax.div(z, BATCH)

    def batch_at(order):
        shift = [0, near, -near, 2][order]
        return lax.rem(first + shift + BATCHES, BATCHES)

    def slots(order):
        return pl.ds(pl.multiple_of(batch_at(order) * rows, rows), rows)

    def out_copy(order, p, part_of):
        return remote(obuf.at[part_of, peer_column(p), slots(order), :], rx.at[part_of, column, slots(order), :],
                      o_send.at[part_of, order, p], o_recv.at[part_of, order, p], in_plane(p))

    def select(order):
        batch = batch_at(order)
        named, weights = [], []
        for i in range(BATCH):
            about = meta[batch * BATCH + i].astype(F32)
            ids, gates = about[0:top, :], about[top:2 * top, :]
            hit = jnp.zeros((Q, tok), F32)
            share = jnp.zeros((Q, tok), F32)
            for k in range(top):
                same = ids[k:k + 1, :] == expert_of
                hit = hit + jnp.where(same, 1.0, 0.0)
                share = share + jnp.where(same, gates[k:k + 1, :], 0.0)
            named.append(hit)
            weights.append(share)
        rank = jnp.dot(jnp.concatenate(named, axis=0).astype(BF), earlier, preferred_element_type=F32)
        for i in range(BATCH):
            key = jnp.where(named[i] > 0.5, rank[i * Q:(i + 1) * Q, :] + float(i * cap), -1.0)
            key_buf[batch * BATCH + i] = key
            chosen = jnp.concatenate(
                [jnp.where(row_of == key[q:q + 1, :], weights[i][q:q + 1, :], 0.0) for q in range(Q)], axis=0
            )
            mt[batch, :, pl.ds(i * tok, tok)] = chosen.astype(BF)
            mtt[batch, pl.ds(i * tok, tok), :] = chosen.T.astype(BF)

    def build_out(order):
        batch = batch_at(order)

        def chunk(n, carry):
            cols = pl.ds(pl.multiple_of(n * 256, 256), 256)
            tokens = cbuf[pl.ds(batch * BATCH, BATCH), :, cols].reshape(BATCH * tok, 256)
            out = jnp.dot(mt[batch], tokens, preferred_element_type=F32).astype(BF)
            inner = pl.ds(pl.multiple_of(lax.rem(n, side // 256) * 256, 256), 256)
            obuf[lax.div(n, side // 256), :, slots(order), inner] = out.reshape(Q, rows, 256)
            return carry

        lax.fori_loop(0, width // 256, chunk, 0)

    def send_out(order, part_of):
        for p in range(1, Q):
            out_copy(order, p, part_of).start()
        rx[part_of, column, slots(order), :] = obuf[part_of, column, slots(order), :]

    def weigh(order):
        batch = batch_at(order)

        def chunk(n, carry):
            cols = pl.ds(pl.multiple_of(n * 256, 256), 256)
            arrived = rbuf[:, slots(order), cols].reshape(Q * rows, 256)
            out = jnp.dot(mtt[batch], arrived, preferred_element_type=F32)
            part[pl.ds(batch * BATCH, BATCH), :, cols] = out.reshape(BATCH, tok, 256)
            return carry

        lax.fori_loop(0, width // 256, chunk, 0)

    def score(order):
        batch = batch_at(order)
        for i in range(BATCH):
            source = batch * BATCH + i
            scores = lax.dot_general(
                rbuf[:, slots(order), :].reshape(Q * rows, width), cbuf[source],
                (((1,), (1,)), ((), ())), preferred_element_type=F32,
            )
            key = key_buf[source]
            ids = meta[source].astype(F32)[0:top, :]
            total = jnp.zeros((top, tok), F32)
            for q in range(Q):
                picked = jnp.where(row_of == key[q:q + 1, :], scores[q * rows:(q + 1) * rows, :], 0.0)
                value = jnp.sum(picked, axis=0, keepdims=True)
                total = total + jnp.where(ids == (z + q * Z).astype(F32), value, 0.0)
            pg[source] = total

    def scatter_copy(way, step, piece):
        span = pl.ds(piece * half, half)
        return remote(rs_out.at[way, step - 1, span, :], rs_in.at[way, step - 1, span, :],
                      rs_send.at[way, step - 1, piece], rs_recv.at[way, step - 1, piece],
                      on_ring(1 if way == 0 else -1))

    def pg_copy(way, step):
        return remote(pg_out.at[way, step - 1], pg_in.at[way, step - 1], pg_send.at[way, step - 1],
                      pg_recv.at[way, step - 1], on_ring(1 if way == 0 else -1))

    def scatter_pieces(step):
        return [(0, 0), (1, 1)] if step == 1 else [(0, 0), (1, 1), (0, 1), (1, 0)]

    def pg_ways(step):
        return [0] if step == 1 else [0, 1]

    def pg_hop(way, step):
        if way not in pg_ways(step):
            return
        value = pg[block(HALF + 1 - step if way == 0 else step - HALF - 1)]
        if step > 1 and way in pg_ways(step - 1):
            pg_copy(way, step - 1).wait_recv()
            value = value + pg_in[way, step - 2]
        pg_out[way, step - 1] = value
        pg_copy(way, step).start()

    def scatter_pair(step, pair, score_step=0):
        for way in (0, 1):
            piece = way if pair == 0 else 1 - way
            there = block(HALF + 1 - step if way == 0 else step - HALF - 1)
            span = pl.ds(piece * half, half)
            value = part[there, span, :]
            if step > 1 and (way, piece) in scatter_pieces(step - 1):
                scatter_copy(way, step - 1, piece).wait_recv()
                value = value + rs_in[way, step - 2, span, :].astype(F32)
            rs_out[way, step - 1, span, :] = value.astype(BF)
            if score_step:
                pg_hop(way, score_step)
            scatter_copy(way, step, piece).start()

    def phi_copy(part_of):
        return remote(phi_out.at[part_of], phi_in.at[part_of], phi_send.at[part_of], phi_recv.at[part_of], partner)

    inner = hidden_ref.shape[1]

    def psi_store(part_of):
        cols = pl.ds(part_of * side, side)
        return pltpu.make_async_copy(psi_ref.at[:, cols], psi_hbm.at[:, cols], local_sem.at[6 + part_of])

    def next_store(part_of):
        cols = pl.ds(part_of * side, side)
        return pltpu.make_async_copy(next_ref.at[:, cols], next_hbm.at[:, cols], local_sem.at[8 + part_of])

    def update(part_of):
        for order in range(BATCHES):
            for p in range(1, Q):
                out_copy(order, p, part_of).wait_recv()
        cols = pl.ds(part_of * side, side)
        for i in range(inner // 128):
            span = pl.ds(i * 128, 128)
            gradient = lax.dot_general(
                hidden_ref[:, span], rx[part_of].reshape(Q * Z * cap, side), (((0,), (0,)), ((), ())),
                preferred_element_type=F32,
            )
            weight = weight_ref[span, cols].astype(F32)
            psi = (weight - STEP_RATE * gradient).astype(BF)
            psi_ref[span, cols] = psi
            own = psi.astype(F32) + (weight - prev_ref[span, cols].astype(F32))
            phi[part_of, span, :] = own
            phi_out[part_of, span, :] = own.astype(BF)
        phi_copy(part_of).start()
        psi_store(part_of).start()

    def mean(part_of):
        phi_copy(part_of).wait_recv()
        cols = pl.ds(part_of * side, side)
        next_ref[:, cols] = (0.5 * (phi[part_of] + phi_in[part_of].astype(F32))).astype(BF)
        next_store(part_of).start()

    gather_pair(2, 0, about=2)
    gather_pair(2, 1, about=3)
    loads[4].wait()
    loads[5].wait()
    gather_pair(3, 0, about=4)
    gather_pair(3, 1, about=5)
    gather_pair(4, 0, about=6)
    gather_pair(4, 1, about=7)
    select(0)
    build_out(0)
    send_out(0, 0)
    gather_pair(5, 0, about=8)
    gather_pair(5, 1)
    meta_copy(0, HALF).wait_recv()
    select(1)
    gather_pair(6, 0)
    gather_pair(6, 1)
    build_out(1)
    send_out(1, 0)
    gather_pair(7, 0)
    gather_pair(7, 1)
    select(2)
    select(3)
    gather_pair(8, 0)
    for way in (0, 1):
        gather_copy(way, HALF - 1, 1 - way).wait_recv()
    build_out(2)
    for p in range(1, Q):
        rows_copy(p).wait_recv()
    weigh(3)
    scatter_pair(1, 0)
    send_out(2, 0)
    weigh(2)
    scatter_pair(2, 1)
    for way, piece in gather_pieces(HALF):
        gather_copy(way, HALF, piece).wait_recv()
    build_out(3)
    send_out(3, 0)
    scatter_pair(2, 0)
    send_out(0, 1)
    send_out(1, 1)
    scatter_pair(3, 1)
    send_out(2, 1)
    send_out(3, 1)
    scatter_pair(3, 0)
    weigh(1)
    score(3)
    scatter_pair(4, 1, score_step=1)
    score(2)
    scatter_pair(4, 0, score_step=2)
    update(0)
    scatter_pair(5, 1, score_step=3)
    score(1)
    scatter_pair(5, 0, score_step=4)
    weigh(0)
    scatter_pair(6, 1, score_step=5)
    score(0)
    scatter_pair(6, 0, score_step=6)
    scatter_pair(7, 1, score_step=7)
    scatter_pair(7, 0, score_step=8)
    update(1)
    scatter_pair(8, 1)
    mean(0)
    scatter_pair(8, 0)
    mean(1)
    for way in pg_ways(HALF):
        pg_copy(way, HALF).wait_recv()
    prob_ref[...] = pg[z] + pg_in[0, HALF - 1] + pg_in[1, HALF - 1]
    for pair in (1, 0):
        for way in (0, 1):
            scatter_copy(way, HALF, way if pair == 0 else 1 - way).wait_recv()
    mixed_ref[...] = (
        part[z] + rs_in[0, HALF - 1].astype(F32) + rs_in[1, HALF - 1].astype(F32)
    ).astype(BF)

    for step in range(1, HALF + 1):
        for way, piece in gather_pieces(step):
            gather_copy(way, step, piece).wait_send()
        for way in meta_ways(step):
            meta_copy(way, step).wait_send()
        for way, piece in scatter_pieces(step):
            scatter_copy(way, step, piece).wait_send()
        for way in pg_ways(step):
            pg_copy(way, step).wait_send()
    for p in range(1, Q):
        rows_copy(p).wait_send()
        for order in range(BATCHES):
            for part_of in range(2):
                out_copy(order, p, part_of).wait_send()
    for part_of in range(2):
        phi_copy(part_of).wait_send()
        psi_store(part_of).wait()
        next_store(part_of).wait()


def hand_out(*refs):
    count = (len(refs) - 1) // 3
    sem = refs[-1]
    operands, results, held = refs[:count], refs[count:2 * count], refs[2 * count:3 * count]
    into = [pltpu.make_async_copy(operands[i], held[i], sem.at[0, i]) for i in range(count)]
    out = [pltpu.make_async_copy(held[i], results[i], sem.at[1, i]) for i in range(count)]
    for copy in into:
        copy.start()
    for i in range(count):
        into[i].wait()
        out[i].start()
    for copy in out:
        copy.wait()


def per_device(expert_ids, gate_probs, cotangent, hidden, w_down, psi_prev):
    tok, top = expert_ids.shape[1:]
    width = cotangent.shape[2]
    slot_count, inner = hidden.shape[2:]
    cap = slot_count // (Q * Z)
    rows = BATCH * cap
    vmem, anywhere = pl.BlockSpec(memory_space=pltpu.VMEM), pl.BlockSpec(memory_space=pl.ANY)
    dma = pltpu.SemaphoreType.DMA
    shapes = (
        jax.ShapeDtypeStruct((tok, width), BF),
        jax.ShapeDtypeStruct((top, tok), F32),
        jax.ShapeDtypeStruct((inner, width), BF),
        jax.ShapeDtypeStruct((inner, width), BF),
    )
    made = pl.pallas_call(
        kernel,
        out_shape=shapes,
        in_specs=[anywhere] * 6,
        out_specs=(vmem, vmem, anywhere, anywhere),
        scratch_shapes=[
            pltpu.VMEM((Z, tok, width), BF),
            pltpu.VMEM((Z, 2 * top, tok), BF),
            pltpu.VMEM((Q, Z * cap, width), BF),
            pltpu.VMEM((Q, Z * cap, width), BF),
            pltpu.VMEM((2, Q, Z * cap, width // 2), BF),
            pltpu.VMEM((2, Q, Z * cap, width // 2), BF),
            pltpu.VMEM((BATCHES, Q * rows, BATCH * tok), BF),
            pltpu.VMEM((BATCHES, BATCH * tok, Q * rows), BF),
            pltpu.VMEM((Z, Q, tok), F32),
            pltpu.VMEM((Z, tok, width), F32),
            pltpu.VMEM((Z, top, tok), F32),
            pltpu.VMEM((2, HALF, tok, width), BF),
            pltpu.VMEM((2, HALF, tok, width), BF),
            pltpu.VMEM((2, HALF, top, tok), F32),
            pltpu.VMEM((2, HALF, top, tok), F32),
            pltpu.VMEM((2, inner, width // 2), F32),
            pltpu.VMEM((2, inner, width // 2), BF),
            pltpu.VMEM((2, inner, width // 2), BF),
            pltpu.VMEM((top, tok), jnp.int32),
            pltpu.VMEM((top, tok), F32),
            pltpu.VMEM((slot_count, inner), BF),
            pltpu.VMEM((inner, width), BF),
            pltpu.VMEM((inner, width), BF),
            pltpu.VMEM((inner, width), BF),
            pltpu.VMEM((inner, width), BF),
            dma((2, HALF, 2)), dma((2, HALF, 2)),
            dma((2, HALF)), dma((2, HALF)),
            dma((Q,)), dma((Q,)),
            dma((2, BATCHES, Q)), dma((2, BATCHES, Q)),
            dma((2, HALF, 2)), dma((2, HALF, 2)),
            dma((2, HALF)), dma((2, HALF)),
            dma((2,)), dma((2,)),
            dma((10,)),
        ],
        compiler_params=pltpu.CompilerParams(
            collective_id=0, has_side_effects=True, vmem_limit_bytes=60 * 1024 * 1024,
        ),
    )(expert_ids[0].T, gate_probs[0].T, cotangent[0], hidden[0, 0], w_down[0, 0], psi_prev[0, 0])
    mixed, prob, w_next, psi_next = pl.pallas_call(
        hand_out,
        out_shape=shapes,
        in_specs=[anywhere] * 4,
        out_specs=(anywhere,) * 4,
        scratch_shapes=[pltpu.VMEM(shape.shape, shape.dtype) for shape in shapes] + [dma((2, 4))],
    )(*made)
    return mixed[None], prob.T[None], w_next[None, None], psi_next[None, None]


def solution(mesh):
    return jax.shard_map(
        per_device,
        mesh=mesh,
        in_specs=(
            P("agent", "expert", None),
            P("agent", "expert", None),
            P("agent", "expert", None),
            P("agent", "expert", None, None),
            P("agent", "expert", None, None),
            P("agent", "expert", None, None),
        ),
        out_specs=(
            P("agent", "expert", None),
            P("agent", "expert", None),
            P("agent", "expert", None, None),
            P("agent", "expert", None, None),
        ),
        check_vma=False,
    )
```

```python
import jax
import jax.numpy as jnp
from jax import lax
from jax.experimental import pallas as pl
from jax.experimental.pallas import tpu as pltpu
from jax.sharding import PartitionSpec as P

Z, Y, X = 16, 4, 2
Q = Y * X
BATCH = 4
BATCHES = Z // BATCH
HALF = Z // 2
STEP_RATE = 0.25
BF, F32 = jnp.bfloat16, jnp.float32


def kernel(
    ids_hbm, gates_hbm, cot_ref, hidden_hbm, weight_hbm, prev_hbm,
    mixed_ref, prob_ref, next_ref, psi_ref,
    cbuf, meta, prod, rbuf, obuf, rx, mt, mtt, key_buf, part, pg, rs_out, rs_in, pg_out, pg_in, phi, phi_out, phi_in,
    ids_ref, gates_ref, hidden_ref, weight_ref, prev_ref,
    ag_send, ag_recv, meta_send, meta_recv, r_send, r_recv, o_send, o_recv,
    rs_send, rs_recv, pg_send, pg_recv, phi_send, phi_recv, local_sem,
):
    tok, width = cot_ref.shape
    top = ids_hbm.shape[0]
    cap = hidden_ref.shape[0] // (Q * Z)
    rows = BATCH * cap
    half = tok // 2
    side = width // 2
    agent = lax.axis_index("agent")
    me = lax.axis_index("expert")
    z = lax.rem(me, Z)
    column = lax.div(me, Z)
    x = lax.rem(column, X)
    y = lax.div(column, X)

    def on_ring(offset):
        return {"expert": column * Z + lax.rem(z + offset + Z, Z)}

    def peer_column(p):
        dy, dx = p // X, p % X
        return lax.rem(y + dy, Y) * X + lax.rem(x + dx, X)

    def in_plane(p):
        return {"expert": peer_column(p) * Z + z}

    partner = {"agent": lax.rem(agent + 2, 4)}

    def block(offset):
        return lax.rem(z + offset + 2 * Z, Z)

    barrier = pltpu.get_barrier_semaphore()
    peers = [on_ring(1), on_ring(-1), partner] + [in_plane(p) for p in range(1, Q)]
    for peer in peers:
        pl.semaphore_signal(barrier, inc=1, device_id=peer, device_id_type=pl.DeviceIdType.MESH)

    loads = [
        pltpu.make_async_copy(src, dst, local_sem.at[i])
        for i, (src, dst) in enumerate([
            (ids_hbm, ids_ref), (gates_hbm, gates_ref), (hidden_hbm, hidden_ref), (weight_hbm, weight_ref),
            (cot_ref, cbuf.at[z]), (prev_hbm, prev_ref),
        ])
    ]
    for load in loads:
        load.start()
    pl.semaphore_wait(barrier, len(peers))

    def remote(src, dst, send, recv, peer):
        return pltpu.make_async_remote_copy(
            src_ref=src, dst_ref=dst, send_sem=send, recv_sem=recv, device_id=peer,
            device_id_type=pl.DeviceIdType.MESH,
        )

    def gather_copy(way, step, piece):
        there = block(-(step - 1) if way == 0 else step - 1)
        place = cbuf.at[there, pl.ds(piece * half, half), :]
        src = cot_ref.at[pl.ds(piece * half, half), :] if step == 1 else place
        return remote(src, place, ag_send.at[way, step - 1, piece], ag_recv.at[way, step - 1, piece],
                      on_ring(1 if way == 0 else -1))

    def meta_copy(way, step):
        place = meta.at[block(-(step - 1) if way == 0 else step - 1)]
        return remote(place, place, meta_send.at[way, step - 1], meta_recv.at[way, step - 1],
                      on_ring(1 if way == 0 else -1))

    def gather_pieces(step):
        if step == HALF:
            return [(0, 0), (1, 1)]
        return [(0, 0), (1, 1), (0, 1), (1, 0)]

    def meta_ways(step):
        return [0] if step == HALF else [0, 1]

    def meta_hop(way, step):
        if step > 1 and way in meta_ways(step - 1):
            meta_copy(way, step - 1).wait_recv()
        if way in meta_ways(step):
            meta_copy(way, step).start()

    def gather_pair(step, pair, about=0):
        for way in (0, 1):
            piece = way if pair == 0 else 1 - way
            if step > 1:
                gather_copy(way, step - 1, piece).wait_recv()
            if about:
                meta_hop(way, about)
            gather_copy(way, step, piece).start()

    gather_pair(1, 0)
    loads[0].wait()
    loads[1].wait()
    meta[z, 0:top, :] = ids_ref[...].astype(F32).astype(BF)
    meta[z, top:2 * top, :] = gates_ref[...].astype(BF)
    gather_pair(1, 1, about=1)
    loads[2].wait()
    loads[3].wait()

    def rows_copy(p):
        return remote(prod.at[peer_column(p)], rbuf.at[column], r_send.at[p], r_recv.at[p], in_plane(p))

    def produce(p):
        there = peer_column(p)
        start = pl.multiple_of(there * Z * cap, Z * cap)
        out = jnp.dot(hidden_ref[pl.ds(start, Z * cap), :], weight_ref[...], preferred_element_type=F32).astype(BF)
        if p == 0:
            rbuf[column] = out
        else:
            prod[there] = out
            rows_copy(p).start()

    for p in list(range(1, Q)) + [0]:
        produce(p)

    lane = lax.broadcasted_iota(jnp.int32, (tok, tok), 1)
    sub = lax.broadcasted_iota(jnp.int32, (tok, tok), 0)
    earlier = (sub < lane).astype(F32).astype(BF)
    expert_of = (lax.broadcasted_iota(jnp.int32, (Q, tok), 0) * Z + z).astype(F32)
    row_of = lax.broadcasted_iota(jnp.int32, (rows, tok), 0).astype(F32)

    near = 1 - 2 * lax.div(3 - lax.rem(z, BATCH), 2)
    first = lax.div(z, BATCH)

    def batch_at(order):
        shift = [0, near, -near, 2][order]
        return lax.rem(first + shift + BATCHES, BATCHES)

    def slots(order):
        return pl.ds(pl.multiple_of(batch_at(order) * rows, rows), rows)

    def out_copy(order, p, part_of):
        return remote(obuf.at[part_of, peer_column(p), slots(order), :], rx.at[part_of, column, slots(order), :],
                      o_send.at[part_of, order, p], o_recv.at[part_of, order, p], in_plane(p))

    def select(order):
        batch = batch_at(order)
        named, weights = [], []
        for i in range(BATCH):
            about = meta[batch * BATCH + i].astype(F32)
            ids, gates = about[0:top, :], about[top:2 * top, :]
            hit = jnp.zeros((Q, tok), F32)
            share = jnp.zeros((Q, tok), F32)
            for k in range(top):
                same = ids[k:k + 1, :] == expert_of
                hit = hit + jnp.where(same, 1.0, 0.0)
                share = share + jnp.where(same, gates[k:k + 1, :], 0.0)
            named.append(hit)
            weights.append(share)
        rank = jnp.dot(jnp.concatenate(named, axis=0).astype(BF), earlier, preferred_element_type=F32)
        for i in range(BATCH):
            key = jnp.where(named[i] > 0.5, rank[i * Q:(i + 1) * Q, :] + float(i * cap), -1.0)
            key_buf[batch * BATCH + i] = key
            chosen = jnp.concatenate(
                [jnp.where(row_of == key[q:q + 1, :], weights[i][q:q + 1, :], 0.0) for q in range(Q)], axis=0
            )
            mt[batch, :, pl.ds(i * tok, tok)] = chosen.astype(BF)
            mtt[batch, pl.ds(i * tok, tok), :] = chosen.T.astype(BF)

    def build_out(order):
        batch = batch_at(order)

        def chunk(n, carry):
            cols = pl.ds(pl.multiple_of(n * 256, 256), 256)
            tokens = cbuf[pl.ds(batch * BATCH, BATCH), :, cols].reshape(BATCH * tok, 256)
            out = jnp.dot(mt[batch], tokens, preferred_element_type=F32).astype(BF)
            inner = pl.ds(pl.multiple_of(lax.rem(n, side // 256) * 256, 256), 256)
            obuf[lax.div(n, side // 256), :, slots(order), inner] = out.reshape(Q, rows, 256)
            return carry

        lax.fori_loop(0, width // 256, chunk, 0)

    def send_out(order, part_of):
        for p in range(1, Q):
            out_copy(order, p, part_of).start()
        rx[part_of, column, slots(order), :] = obuf[part_of, column, slots(order), :]

    def weigh(order):
        batch = batch_at(order)

        def chunk(n, carry):
            cols = pl.ds(pl.multiple_of(n * 256, 256), 256)
            arrived = rbuf[:, slots(order), cols].reshape(Q * rows, 256)
            out = jnp.dot(mtt[batch], arrived, preferred_element_type=F32)
            part[pl.ds(batch * BATCH, BATCH), :, cols] = out.reshape(BATCH, tok, 256)
            return carry

        lax.fori_loop(0, width // 256, chunk, 0)

    def score(order):
        batch = batch_at(order)
        for i in range(BATCH):
            source = batch * BATCH + i
            scores = lax.dot_general(
                rbuf[:, slots(order), :].reshape(Q * rows, width), cbuf[source],
                (((1,), (1,)), ((), ())), preferred_element_type=F32,
            )
            key = key_buf[source]
            ids = meta[source].astype(F32)[0:top, :]
            total = jnp.zeros((top, tok), F32)
            for q in range(Q):
                picked = jnp.where(row_of == key[q:q + 1, :], scores[q * rows:(q + 1) * rows, :], 0.0)
                value = jnp.sum(picked, axis=0, keepdims=True)
                total = total + jnp.where(ids == (z + q * Z).astype(F32), value, 0.0)
            pg[source] = total

    def scatter_copy(way, step, piece):
        span = pl.ds(piece * half, half)
        return remote(rs_out.at[way, step - 1, span, :], rs_in.at[way, step - 1, span, :],
                      rs_send.at[way, step - 1, piece], rs_recv.at[way, step - 1, piece],
                      on_ring(1 if way == 0 else -1))

    def pg_copy(way, step):
        return remote(pg_out.at[way, step - 1], pg_in.at[way, step - 1], pg_send.at[way, step - 1],
                      pg_recv.at[way, step - 1], on_ring(1 if way == 0 else -1))

    def scatter_pieces(step):
        return [(0, 0), (1, 1)] if step == 1 else [(0, 0), (1, 1), (0, 1), (1, 0)]

    def pg_ways(step):
        return [0] if step == 1 else [0, 1]

    def pg_hop(way, step):
        if way not in pg_ways(step):
            return
        value = pg[block(HALF + 1 - step if way == 0 else step - HALF - 1)]
        if step > 1 and way in pg_ways(step - 1):
            pg_copy(way, step - 1).wait_recv()
            value = value + pg_in[way, step - 2]
        pg_out[way, step - 1] = value
        pg_copy(way, step).start()

    def scatter_pair(step, pair, score_step=0):
        for way in (0, 1):
            piece = way if pair == 0 else 1 - way
            there = block(HALF + 1 - step if way == 0 else step - HALF - 1)
            span = pl.ds(piece * half, half)
            value = part[there, span, :]
            if step > 1 and (way, piece) in scatter_pieces(step - 1):
                scatter_copy(way, step - 1, piece).wait_recv()
                value = value + rs_in[way, step - 2, span, :].astype(F32)
            rs_out[way, step - 1, span, :] = value.astype(BF)
            if score_step:
                pg_hop(way, score_step)
            scatter_copy(way, step, piece).start()

    def phi_copy(part_of):
        return remote(phi_out.at[part_of], phi_in.at[part_of], phi_send.at[part_of], phi_recv.at[part_of], partner)

    inner = hidden_ref.shape[1]

    def update(part_of):
        for order in range(BATCHES):
            for p in range(1, Q):
                out_copy(order, p, part_of).wait_recv()
        cols = pl.ds(part_of * side, side)
        for i in range(inner // 128):
            span = pl.ds(i * 128, 128)
            gradient = lax.dot_general(
                hidden_ref[:, span], rx[part_of].reshape(Q * Z * cap, side), (((0,), (0,)), ((), ())),
                preferred_element_type=F32,
            )
            weight = weight_ref[span, cols].astype(F32)
            psi = (weight - STEP_RATE * gradient).astype(BF)
            psi_ref[span, cols] = psi
            own = psi.astype(F32) + (weight - prev_ref[span, cols].astype(F32))
            phi[part_of, span, :] = own
            phi_out[part_of, span, :] = own.astype(BF)
        phi_copy(part_of).start()

    def mean(part_of):
        phi_copy(part_of).wait_recv()
        cols = pl.ds(part_of * side, side)
        next_ref[:, cols] = (0.5 * (phi[part_of] + phi_in[part_of].astype(F32))).astype(BF)

    gather_pair(2, 0, about=2)
    gather_pair(2, 1, about=3)
    loads[4].wait()
    loads[5].wait()
    gather_pair(3, 0, about=4)
    gather_pair(3, 1, about=5)
    gather_pair(4, 0, about=6)
    gather_pair(4, 1, about=7)
    select(0)
    build_out(0)
    send_out(0, 0)
    gather_pair(5, 0, about=8)
    gather_pair(5, 1)
    meta_copy(0, HALF).wait_recv()
    select(1)
    gather_pair(6, 0)
    gather_pair(6, 1)
    build_out(1)
    send_out(1, 0)
    gather_pair(7, 0)
    gather_pair(7, 1)
    select(2)
    select(3)
    gather_pair(8, 0)
    for way in (0, 1):
        gather_copy(way, HALF - 1, 1 - way).wait_recv()
    build_out(2)
    for p in range(1, Q):
        rows_copy(p).wait_recv()
    weigh(3)
    scatter_pair(1, 0)
    send_out(2, 0)
    weigh(2)
    scatter_pair(2, 1)
    for way, piece in gather_pieces(HALF):
        gather_copy(way, HALF, piece).wait_recv()
    build_out(3)
    send_out(3, 0)
    scatter_pair(2, 0)
    send_out(0, 1)
    send_out(1, 1)
    scatter_pair(3, 1)
    send_out(2, 1)
    send_out(3, 1)
    scatter_pair(3, 0)
    weigh(1)
    score(3)
    scatter_pair(4, 1, score_step=1)
    score(2)
    scatter_pair(4, 0, score_step=2)
    update(0)
    scatter_pair(5, 1, score_step=3)
    score(1)
    scatter_pair(5, 0, score_step=4)
    weigh(0)
    scatter_pair(6, 1, score_step=5)
    score(0)
    scatter_pair(6, 0, score_step=6)
    scatter_pair(7, 1, score_step=7)
    scatter_pair(7, 0, score_step=8)
    update(1)
    scatter_pair(8, 1)
    mean(0)
    scatter_pair(8, 0)
    mean(1)
    for way in pg_ways(HALF):
        pg_copy(way, HALF).wait_recv()
    prob_ref[...] = pg[z] + pg_in[0, HALF - 1] + pg_in[1, HALF - 1]
    for pair in (1, 0):
        for way in (0, 1):
            scatter_copy(way, HALF, way if pair == 0 else 1 - way).wait_recv()
    mixed_ref[...] = (
        part[z] + rs_in[0, HALF - 1].astype(F32) + rs_in[1, HALF - 1].astype(F32)
    ).astype(BF)

    for step in range(1, HALF + 1):
        for way, piece in gather_pieces(step):
            gather_copy(way, step, piece).wait_send()
        for way in meta_ways(step):
            meta_copy(way, step).wait_send()
        for way, piece in scatter_pieces(step):
            scatter_copy(way, step, piece).wait_send()
        for way in pg_ways(step):
            pg_copy(way, step).wait_send()
    for p in range(1, Q):
        rows_copy(p).wait_send()
        for order in range(BATCHES):
            for part_of in range(2):
                out_copy(order, p, part_of).wait_send()
    for part_of in range(2):
        phi_copy(part_of).wait_send()


def hand_out(*refs):
    count = (len(refs) - 1) // 2
    sem = refs[-1]
    copies = [pltpu.make_async_copy(refs[i], refs[count + i], sem.at[i]) for i in range(count)]
    for copy in copies:
        copy.start()
    for copy in copies:
        copy.wait()


def per_device(expert_ids, gate_probs, cotangent, hidden, w_down, psi_prev):
    tok, top = expert_ids.shape[1:]
    width = cotangent.shape[2]
    slot_count, inner = hidden.shape[2:]
    cap = slot_count // (Q * Z)
    rows = BATCH * cap
    vmem, anywhere = pl.BlockSpec(memory_space=pltpu.VMEM), pl.BlockSpec(memory_space=pl.ANY)
    dma = pltpu.SemaphoreType.DMA
    shapes = (
        jax.ShapeDtypeStruct((tok, width), BF),
        jax.ShapeDtypeStruct((top, tok), F32),
        jax.ShapeDtypeStruct((inner, width), BF),
        jax.ShapeDtypeStruct((inner, width), BF),
    )
    made = pl.pallas_call(
        kernel,
        out_shape=tuple(pltpu.VMEM(shape.shape, shape.dtype) for shape in shapes),
        in_specs=[anywhere] * 6,
        out_specs=(vmem,) * 4,
        scratch_shapes=[
            pltpu.VMEM((Z, tok, width), BF),
            pltpu.VMEM((Z, 2 * top, tok), BF),
            pltpu.VMEM((Q, Z * cap, width), BF),
            pltpu.VMEM((Q, Z * cap, width), BF),
            pltpu.VMEM((2, Q, Z * cap, width // 2), BF),
            pltpu.VMEM((2, Q, Z * cap, width // 2), BF),
            pltpu.VMEM((BATCHES, Q * rows, BATCH * tok), BF),
            pltpu.VMEM((BATCHES, BATCH * tok, Q * rows), BF),
            pltpu.VMEM((Z, Q, tok), F32),
            pltpu.VMEM((Z, tok, width), F32),
            pltpu.VMEM((Z, top, tok), F32),
            pltpu.VMEM((2, HALF, tok, width), BF),
            pltpu.VMEM((2, HALF, tok, width), BF),
            pltpu.VMEM((2, HALF, top, tok), F32),
            pltpu.VMEM((2, HALF, top, tok), F32),
            pltpu.VMEM((2, inner, width // 2), F32),
            pltpu.VMEM((2, inner, width // 2), BF),
            pltpu.VMEM((2, inner, width // 2), BF),
            pltpu.VMEM((top, tok), jnp.int32),
            pltpu.VMEM((top, tok), F32),
            pltpu.VMEM((slot_count, inner), BF),
            pltpu.VMEM((inner, width), BF),
            pltpu.VMEM((inner, width), BF),
            dma((2, HALF, 2)), dma((2, HALF, 2)),
            dma((2, HALF)), dma((2, HALF)),
            dma((Q,)), dma((Q,)),
            dma((2, BATCHES, Q)), dma((2, BATCHES, Q)),
            dma((2, HALF, 2)), dma((2, HALF, 2)),
            dma((2, HALF)), dma((2, HALF)),
            dma((2,)), dma((2,)),
            dma((6,)),
        ],
        compiler_params=pltpu.CompilerParams(
            collective_id=0, has_side_effects=True, vmem_limit_bytes=60 * 1024 * 1024,
        ),
    )(expert_ids[0].T, gate_probs[0].T, cotangent[0], hidden[0, 0], w_down[0, 0], psi_prev[0, 0])
    mixed, prob, w_next, psi_next = pl.pallas_call(
        hand_out,
        out_shape=shapes,
        in_specs=[anywhere] * 4,
        out_specs=(anywhere,) * 4,
        scratch_shapes=[dma((4,))],
    )(*(pltpu.with_memory_space_constraint(part, pltpu.VMEM) for part in made))
    return mixed[None], prob.T[None], w_next[None, None], psi_next[None, None]


def solution(mesh):
    return jax.shard_map(
        per_device,
        mesh=mesh,
        in_specs=(
            P("agent", "expert", None),
            P("agent", "expert", None),
            P("agent", "expert", None),
            P("agent", "expert", None, None),
            P("agent", "expert", None, None),
            P("agent", "expert", None, None),
        ),
        out_specs=(
            P("agent", "expert", None),
            P("agent", "expert", None),
            P("agent", "expert", None, None),
            P("agent", "expert", None, None),
        ),
        check_vma=False,
    )
```

```python
import jax
import jax.numpy as jnp
from jax import lax
from jax.experimental import pallas as pl
from jax.experimental.pallas import tpu as pltpu
from jax.sharding import PartitionSpec as P

Z, Y, X = 16, 4, 2
Q = Y * X
BATCH = 4
BATCHES = Z // BATCH
HALF = Z // 2
STEP_RATE = 0.25
BF, F32 = jnp.bfloat16, jnp.float32


def kernel(
    ids_hbm, gates_hbm, cot_ref, hidden_hbm, weight_hbm, prev_hbm,
    mixed_ref, prob_ref, next_ref, psi_ref,
    cbuf, meta, prod, rbuf, obuf, rx, mt, mtt, key_buf, part, pg, rs_out, rs_in, pg_out, pg_in, phi, phi_out, phi_in,
    ids_ref, gates_ref, hidden_ref, weight_ref, prev_ref,
    ag_send, ag_recv, meta_send, meta_recv, r_send, r_recv, o_send, o_recv,
    rs_send, rs_recv, pg_send, pg_recv, phi_send, phi_recv, local_sem,
):
    tok, width = cot_ref.shape
    top = ids_hbm.shape[0]
    cap = hidden_ref.shape[0] // (Q * Z)
    rows = BATCH * cap
    half = tok // 2
    side = width // 2
    agent = lax.axis_index("agent")
    me = lax.axis_index("expert")
    z = lax.rem(me, Z)
    column = lax.div(me, Z)
    x = lax.rem(column, X)
    y = lax.div(column, X)

    def on_ring(offset):
        return {"expert": column * Z + lax.rem(z + offset + Z, Z)}

    def peer_column(p):
        dy, dx = p // X, p % X
        return lax.rem(y + dy, Y) * X + lax.rem(x + dx, X)

    def in_plane(p):
        return {"expert": peer_column(p) * Z + z}

    partner = {"agent": lax.rem(agent + 2, 4)}

    def block(offset):
        return lax.rem(z + offset + 2 * Z, Z)

    barrier = pltpu.get_barrier_semaphore()
    peers = [on_ring(1), on_ring(-1), partner] + [in_plane(p) for p in range(1, Q)]
    for peer in peers:
        pl.semaphore_signal(barrier, inc=1, device_id=peer, device_id_type=pl.DeviceIdType.MESH)

    loads = [
        pltpu.make_async_copy(src, dst, local_sem.at[i])
        for i, (src, dst) in enumerate([
            (ids_hbm, ids_ref), (gates_hbm, gates_ref), (hidden_hbm, hidden_ref), (weight_hbm, weight_ref),
            (cot_ref, cbuf.at[z]), (prev_hbm, prev_ref),
        ])
    ]
    for load in loads:
        load.start()
    pl.semaphore_wait(barrier, len(peers))

    def remote(src, dst, send, recv, peer):
        return pltpu.make_async_remote_copy(
            src_ref=src, dst_ref=dst, send_sem=send, recv_sem=recv, device_id=peer,
            device_id_type=pl.DeviceIdType.MESH,
        )

    def gather_copy(way, step, piece):
        there = block(-(step - 1) if way == 0 else step - 1)
        place = cbuf.at[there, pl.ds(piece * half, half), :]
        src = cot_ref.at[pl.ds(piece * half, half), :] if step == 1 else place
        return remote(src, place, ag_send.at[way, step - 1, piece], ag_recv.at[way, step - 1, piece],
                      on_ring(1 if way == 0 else -1))

    def meta_copy(way, step):
        place = meta.at[block(-(step - 1) if way == 0 else step - 1)]
        return remote(place, place, meta_send.at[way, step - 1], meta_recv.at[way, step - 1],
                      on_ring(1 if way == 0 else -1))

    def gather_pieces(step):
        if step == HALF:
            return [(0, 0), (1, 1)]
        return [(0, 0), (1, 1), (0, 1), (1, 0)]

    def meta_ways(step):
        return [0] if step == HALF else [0, 1]

    def meta_hop(way, step):
        if step > 1 and way in meta_ways(step - 1):
            meta_copy(way, step - 1).wait_recv()
        if way in meta_ways(step):
            meta_copy(way, step).start()

    def gather_pair(step, pair, about=0):
        for way in (0, 1):
            piece = way if pair == 0 else 1 - way
            if step > 1:
                gather_copy(way, step - 1, piece).wait_recv()
            if about:
                meta_hop(way, about)
            gather_copy(way, step, piece).start()

    gather_pair(1, 0)
    loads[0].wait()
    loads[1].wait()
    meta[z, 0:top, :] = ids_ref[...].astype(F32).astype(BF)
    meta[z, top:2 * top, :] = gates_ref[...].astype(BF)
    gather_pair(1, 1, about=1)
    loads[2].wait()
    loads[3].wait()

    near = 1 - 2 * lax.div(3 - lax.rem(z, BATCH), 2)
    first = lax.div(z, BATCH)

    def batch_at(order):
        shift = [0, near, -near, 2][order]
        return lax.rem(first + shift + BATCHES, BATCHES)

    def slots(order):
        return pl.ds(pl.multiple_of(batch_at(order) * rows, rows), rows)

    def rows_copy(order, p):
        return remote(prod.at[peer_column(p), slots(order), :], rbuf.at[column, slots(order), :],
                      r_send.at[order, p], r_recv.at[order, p], in_plane(p))

    def rows_arrive(order):
        for p in range(1, Q):
            rows_copy(order, p).wait_recv()

    def produce(p):
        there = peer_column(p)
        start = pl.multiple_of(there * Z * cap, Z * cap)
        out = jnp.dot(hidden_ref[pl.ds(start, Z * cap), :], weight_ref[...], preferred_element_type=F32).astype(BF)
        if p == 0:
            rbuf[column] = out
        else:
            prod[there] = out
            rows_copy(3, p).start()
            rows_copy(2, p).start()

    for p in list(range(1, Q)) + [0]:
        produce(p)
    for order in (1, 0):
        for p in range(1, Q):
            rows_copy(order, p).start()

    lane = lax.broadcasted_iota(jnp.int32, (tok, tok), 1)
    sub = lax.broadcasted_iota(jnp.int32, (tok, tok), 0)
    earlier = (sub < lane).astype(F32).astype(BF)
    expert_of = (lax.broadcasted_iota(jnp.int32, (Q, tok), 0) * Z + z).astype(F32)
    row_of = lax.broadcasted_iota(jnp.int32, (rows, tok), 0).astype(F32)

    def out_copy(order, p, part_of):
        return remote(obuf.at[part_of, peer_column(p), slots(order), :], rx.at[part_of, column, slots(order), :],
                      o_send.at[part_of, order, p], o_recv.at[part_of, order, p], in_plane(p))

    def select(order):
        batch = batch_at(order)
        named, weights = [], []
        for i in range(BATCH):
            about = meta[batch * BATCH + i].astype(F32)
            ids, gates = about[0:top, :], about[top:2 * top, :]
            hit = jnp.zeros((Q, tok), F32)
            share = jnp.zeros((Q, tok), F32)
            for k in range(top):
                same = ids[k:k + 1, :] == expert_of
                hit = hit + jnp.where(same, 1.0, 0.0)
                share = share + jnp.where(same, gates[k:k + 1, :], 0.0)
            named.append(hit)
            weights.append(share)
        rank = jnp.dot(jnp.concatenate(named, axis=0).astype(BF), earlier, preferred_element_type=F32)
        for i in range(BATCH):
            key = jnp.where(named[i] > 0.5, rank[i * Q:(i + 1) * Q, :] + float(i * cap), -1.0)
            key_buf[batch * BATCH + i] = key
            chosen = jnp.concatenate(
                [jnp.where(row_of == key[q:q + 1, :], weights[i][q:q + 1, :], 0.0) for q in range(Q)], axis=0
            )
            mt[batch, :, pl.ds(i * tok, tok)] = chosen.astype(BF)
            mtt[batch, pl.ds(i * tok, tok), :] = chosen.T.astype(BF)

    def build_out(order):
        batch = batch_at(order)

        def chunk(n, carry):
            cols = pl.ds(pl.multiple_of(n * 256, 256), 256)
            tokens = cbuf[pl.ds(batch * BATCH, BATCH), :, cols].reshape(BATCH * tok, 256)
            out = jnp.dot(mt[batch], tokens, preferred_element_type=F32).astype(BF)
            inner = pl.ds(pl.multiple_of(lax.rem(n, side // 256) * 256, 256), 256)
            obuf[lax.div(n, side // 256), :, slots(order), inner] = out.reshape(Q, rows, 256)
            return carry

        lax.fori_loop(0, width // 256, chunk, 0)

    def send_out(order, part_of):
        for p in range(1, Q):
            out_copy(order, p, part_of).start()
        rx[part_of, column, slots(order), :] = obuf[part_of, column, slots(order), :]

    def weigh(order):
        batch = batch_at(order)

        def chunk(n, carry):
            cols = pl.ds(pl.multiple_of(n * 256, 256), 256)
            arrived = rbuf[:, slots(order), cols].reshape(Q * rows, 256)
            out = jnp.dot(mtt[batch], arrived, preferred_element_type=F32)
            part[pl.ds(batch * BATCH, BATCH), :, cols] = out.reshape(BATCH, tok, 256)
            return carry

        lax.fori_loop(0, width // 256, chunk, 0)

    def score(order):
        batch = batch_at(order)
        for i in range(BATCH):
            source = batch * BATCH + i
            scores = lax.dot_general(
                rbuf[:, slots(order), :].reshape(Q * rows, width), cbuf[source],
                (((1,), (1,)), ((), ())), preferred_element_type=F32,
            )
            key = key_buf[source]
            ids = meta[source].astype(F32)[0:top, :]
            total = jnp.zeros((top, tok), F32)
            for q in range(Q):
                picked = jnp.where(row_of == key[q:q + 1, :], scores[q * rows:(q + 1) * rows, :], 0.0)
                value = jnp.sum(picked, axis=0, keepdims=True)
                total = total + jnp.where(ids == (z + q * Z).astype(F32), value, 0.0)
            pg[source] = total

    def scatter_copy(way, step, piece):
        span = pl.ds(piece * half, half)
        return remote(rs_out.at[way, step - 1, span, :], rs_in.at[way, step - 1, span, :],
                      rs_send.at[way, step - 1, piece], rs_recv.at[way, step - 1, piece],
                      on_ring(1 if way == 0 else -1))

    def pg_copy(way, step):
        return remote(pg_out.at[way, step - 1], pg_in.at[way, step - 1], pg_send.at[way, step - 1],
                      pg_recv.at[way, step - 1], on_ring(1 if way == 0 else -1))

    def scatter_pieces(step):
        return [(0, 0), (1, 1)] if step == 1 else [(0, 0), (1, 1), (0, 1), (1, 0)]

    def pg_ways(step):
        return [0] if step == 1 else [0, 1]

    def pg_hop(way, step):
        if way not in pg_ways(step):
            return
        value = pg[block(HALF + 1 - step if way == 0 else step - HALF - 1)]
        if step > 1 and way in pg_ways(step - 1):
            pg_copy(way, step - 1).wait_recv()
            value = value + pg_in[way, step - 2]
        pg_out[way, step - 1] = value
        pg_copy(way, step).start()

    def scatter_pair(step, pair, score_step=0):
        for way in (0, 1):
            piece = way if pair == 0 else 1 - way
            there = block(HALF + 1 - step if way == 0 else step - HALF - 1)
            span = pl.ds(piece * half, half)
            value = part[there, span, :]
            if step > 1 and (way, piece) in scatter_pieces(step - 1):
                scatter_copy(way, step - 1, piece).wait_recv()
                value = value + rs_in[way, step - 2, span, :].astype(F32)
            rs_out[way, step - 1, span, :] = value.astype(BF)
            if score_step:
                pg_hop(way, score_step)
            scatter_copy(way, step, piece).start()

    def phi_copy(part_of):
        return remote(phi_out.at[part_of], phi_in.at[part_of], phi_send.at[part_of], phi_recv.at[part_of], partner)

    inner = hidden_ref.shape[1]

    def update(part_of):
        for order in range(BATCHES):
            for p in range(1, Q):
                out_copy(order, p, part_of).wait_recv()
        cols = pl.ds(part_of * side, side)
        for i in range(inner // 128):
            span = pl.ds(i * 128, 128)
            gradient = lax.dot_general(
                hidden_ref[:, span], rx[part_of].reshape(Q * Z * cap, side), (((0,), (0,)), ((), ())),
                preferred_element_type=F32,
            )
            weight = weight_ref[span, cols].astype(F32)
            psi = (weight - STEP_RATE * gradient).astype(BF)
            psi_ref[span, cols] = psi
            own = psi.astype(F32) + (weight - prev_ref[span, cols].astype(F32))
            phi[part_of, span, :] = own
            phi_out[part_of, span, :] = own.astype(BF)
        phi_copy(part_of).start()

    def mean(part_of):
        phi_copy(part_of).wait_recv()
        cols = pl.ds(part_of * side, side)
        next_ref[:, cols] = (0.5 * (phi[part_of] + phi_in[part_of].astype(F32))).astype(BF)

    gather_pair(2, 0, about=2)
    gather_pair(2, 1, about=3)
    loads[4].wait()
    loads[5].wait()
    gather_pair(3, 0, about=4)
    gather_pair(3, 1, about=5)
    gather_pair(4, 0, about=6)
    gather_pair(4, 1, about=7)
    select(0)
    build_out(0)
    send_out(0, 0)
    gather_pair(5, 0, about=8)
    gather_pair(5, 1)
    meta_copy(0, HALF).wait_recv()
    select(1)
    gather_pair(6, 0)
    select(3)
    gather_pair(6, 1)
    build_out(1)
    send_out(1, 0)
    gather_pair(7, 0)
    select(2)
    rows_arrive(3)
    weigh(3)
    gather_pair(7, 1)
    rows_arrive(2)
    weigh(2)
    gather_pair(8, 0)
    scatter_pair(1, 0)
    scatter_pair(2, 1)
    for way in (0, 1):
        gather_copy(way, HALF - 1, 1 - way).wait_recv()
    build_out(2)
    send_out(2, 0)
    for way, piece in gather_pieces(HALF):
        gather_copy(way, HALF, piece).wait_recv()
    build_out(3)
    send_out(3, 0)
    scatter_pair(2, 0)
    send_out(0, 1)
    send_out(1, 1)
    scatter_pair(3, 1)
    send_out(2, 1)
    send_out(3, 1)
    scatter_pair(3, 0)
    rows_arrive(1)
    weigh(1)
    score(3)
    scatter_pair(4, 1, score_step=1)
    score(2)
    scatter_pair(4, 0, score_step=2)
    update(0)
    scatter_pair(5, 1, score_step=3)
    score(1)
    scatter_pair(5, 0, score_step=4)
    rows_arrive(0)
    weigh(0)
    scatter_pair(6, 1, score_step=5)
    score(0)
    scatter_pair(6, 0, score_step=6)
    scatter_pair(7, 1, score_step=7)
    scatter_pair(7, 0, score_step=8)
    update(1)
    scatter_pair(8, 1)
    mean(0)
    scatter_pair(8, 0)
    mean(1)
    for way in pg_ways(HALF):
        pg_copy(way, HALF).wait_recv()
    prob_ref[...] = pg[z] + pg_in[0, HALF - 1] + pg_in[1, HALF - 1]
    for pair in (1, 0):
        for way in (0, 1):
            scatter_copy(way, HALF, way if pair == 0 else 1 - way).wait_recv()
    mixed_ref[...] = (
        part[z] + rs_in[0, HALF - 1].astype(F32) + rs_in[1, HALF - 1].astype(F32)
    ).astype(BF)

    for step in range(1, HALF + 1):
        for way, piece in gather_pieces(step):
            gather_copy(way, step, piece).wait_send()
        for way in meta_ways(step):
            meta_copy(way, step).wait_send()
        for way, piece in scatter_pieces(step):
            scatter_copy(way, step, piece).wait_send()
        for way in pg_ways(step):
            pg_copy(way, step).wait_send()
    for p in range(1, Q):
        for order in range(BATCHES):
            rows_copy(order, p).wait_send()
            for part_of in range(2):
                out_copy(order, p, part_of).wait_send()
    for part_of in range(2):
        phi_copy(part_of).wait_send()


def hand_out(*refs):
    count = (len(refs) - 1) // 2
    sem = refs[-1]
    copies = [pltpu.make_async_copy(refs[i], refs[count + i], sem.at[i]) for i in range(count)]
    for copy in copies:
        copy.start()
    for copy in copies:
        copy.wait()


def per_device(expert_ids, gate_probs, cotangent, hidden, w_down, psi_prev):
    tok, top = expert_ids.shape[1:]
    width = cotangent.shape[2]
    slot_count, inner = hidden.shape[2:]
    cap = slot_count // (Q * Z)
    rows = BATCH * cap
    vmem, anywhere = pl.BlockSpec(memory_space=pltpu.VMEM), pl.BlockSpec(memory_space=pl.ANY)
    dma = pltpu.SemaphoreType.DMA
    shapes = (
        jax.ShapeDtypeStruct((tok, width), BF),
        jax.ShapeDtypeStruct((top, tok), F32),
        jax.ShapeDtypeStruct((inner, width), BF),
        jax.ShapeDtypeStruct((inner, width), BF),
    )
    made = pl.pallas_call(
        kernel,
        out_shape=tuple(pltpu.VMEM(shape.shape, shape.dtype) for shape in shapes),
        in_specs=[anywhere] * 6,
        out_specs=(vmem,) * 4,
        scratch_shapes=[
            pltpu.VMEM((Z, tok, width), BF),
            pltpu.VMEM((Z, 2 * top, tok), BF),
            pltpu.VMEM((Q, Z * cap, width), BF),
            pltpu.VMEM((Q, Z * cap, width), BF),
            pltpu.VMEM((2, Q, Z * cap, width // 2), BF),
            pltpu.VMEM((2, Q, Z * cap, width // 2), BF),
            pltpu.VMEM((BATCHES, Q * rows, BATCH * tok), BF),
            pltpu.VMEM((BATCHES, BATCH * tok, Q * rows), BF),
            pltpu.VMEM((Z, Q, tok), F32),
            pltpu.VMEM((Z, tok, width), F32),
            pltpu.VMEM((Z, top, tok), F32),
            pltpu.VMEM((2, HALF, tok, width), BF),
            pltpu.VMEM((2, HALF, tok, width), BF),
            pltpu.VMEM((2, HALF, top, tok), F32),
            pltpu.VMEM((2, HALF, top, tok), F32),
            pltpu.VMEM((2, inner, width // 2), F32),
            pltpu.VMEM((2, inner, width // 2), BF),
            pltpu.VMEM((2, inner, width // 2), BF),
            pltpu.VMEM((top, tok), jnp.int32),
            pltpu.VMEM((top, tok), F32),
            pltpu.VMEM((slot_count, inner), BF),
            pltpu.VMEM((inner, width), BF),
            pltpu.VMEM((inner, width), BF),
            dma((2, HALF, 2)), dma((2, HALF, 2)),
            dma((2, HALF)), dma((2, HALF)),
            dma((BATCHES, Q)), dma((BATCHES, Q)),
            dma((2, BATCHES, Q)), dma((2, BATCHES, Q)),
            dma((2, HALF, 2)), dma((2, HALF, 2)),
            dma((2, HALF)), dma((2, HALF)),
            dma((2,)), dma((2,)),
            dma((6,)),
        ],
        compiler_params=pltpu.CompilerParams(
            collective_id=0, has_side_effects=True, vmem_limit_bytes=60 * 1024 * 1024,
        ),
    )(expert_ids[0].T, gate_probs[0].T, cotangent[0], hidden[0, 0], w_down[0, 0], psi_prev[0, 0])
    mixed, prob, w_next, psi_next = pl.pallas_call(
        hand_out,
        out_shape=shapes,
        in_specs=[anywhere] * 4,
        out_specs=(anywhere,) * 4,
        scratch_shapes=[dma((4,))],
    )(*(pltpu.with_memory_space_constraint(part, pltpu.VMEM) for part in made))
    return mixed[None], prob.T[None], w_next[None, None], psi_next[None, None]


def solution(mesh):
    return jax.shard_map(
        per_device,
        mesh=mesh,
        in_specs=(
            P("agent", "expert", None),
            P("agent", "expert", None),
            P("agent", "expert", None),
            P("agent", "expert", None, None),
            P("agent", "expert", None, None),
            P("agent", "expert", None, None),
        ),
        out_specs=(
            P("agent", "expert", None),
            P("agent", "expert", None),
            P("agent", "expert", None, None),
            P("agent", "expert", None, None),
        ),
        check_vma=False,
    )
```
